32 devices in a mesh: section: 8 (over z, core), req: 4 (over y, x).
Axes of the slice: x: 2, y: 2, z: 4, core: 2. Of those that a mesh axis runs over, the one named last changes fastest.
Arguments:
- latents: bfloat16 [128, 3072], P('req'), may hold values from -6 to 6
- patch_route: int32 [128], replicated, may hold values from 0 to 127, each once
- request_len: int32 [16], replicated, may hold values from 1 to 32, 128 in all
- span_order: int32 [2], replicated, may hold values from 0 to 1, each once
- modulation: float32 [8, 16, 3, 3072], P('section'), may hold values from -4 to 4
- w_qkv: bfloat16 [8, 3072, 16, 384], P('section', None, 'req'), may hold values from -0.109375 to 0.109375
- w_mlp_in: bfloat16 [8, 3072, 6144], P('section', None, 'req'), may hold values from -0.109375 to 0.109375
- w_out_attn: bfloat16 [8, 16, 128, 3072], P('section', 'req'), may hold values from -0.0625 to 0.0625
- w_out_mlp: bfloat16 [8, 6144, 3072], P('section', 'req'), may hold values from -0.0625 to 0.0625
- stale_kv: bfloat16 [8, 128, 16, 256], P('section', None, 'req'), may hold values from -160 to 160
Outputs:
- denoised: bfloat16 [128, 3072], P('req', 'section')
The draws below stay inside these ranges and needn't reach their ends.
All inputs are finite; a program needn't handle non-finite values.
Results may differ from the reference program's by a relative error of at most 0.04.
Values may be sent and summed in bfloat16 or wider, within the bound.
A program may use at most 128 MiB of HBM per device.

```python
import math
import jax
import jax.numpy as jnp
import numpy as np
from jax import lax

D = 3072
HEADS = 16
HD = 128
MLP = 6144
PATCHES = 128
SPANS = 2
REQS = 16
MOST = 32
SECTIONS = 8
N_REQ = 4


def draw_stale_kv(key, part):
    key = jax.random.fold_in(key, 7)
    shape = (SECTIONS, PATCHES, HEADS, 2 * HD)
    base = jnp.clip(jax.random.normal(key, shape, jnp.float32), -4.0, 4.0)
    return base.astype(jnp.bfloat16)


def steps_of(key, shape, shards, smallest, high):
    def one(dim, shards_of):
        steps = jax.random.uniform(jax.random.fold_in(jax.random.fold_in(key, 6), dim), (shards_of,), jnp.float32, smallest / len(shards), high / len(shards))
        return jnp.repeat(jnp.exp(steps), shape[dim] // shards_of).reshape((-1,) + (1,) * (len(shape) - dim - 1))

    factor_of = one(*shards[0])
    for cut in shards[1:]:
        factor_of = factor_of * one(*cut)
    return factor_of


def profile(count, total, most, skew):
    portions = [(1 << 20) // math.isqrt(standing ** skew) + 1 for standing in range(2, count + 1)]
    surplus, counts = total - most - (count - 1), [1] * (count - 1)
    while surplus > 0:
        movable = [i for i in range(count - 1) if counts[i] < most]
        mass, left = sum([portions[i] for i in movable]), surplus
        for i in movable:
            addition = min(most - counts[i], max(1, left * portions[i] // mass), surplus)
            counts[i] = counts[i] + addition
            surplus = surplus - addition
    return np.array([most] + counts)


def ragged(own_key, number_of, total, reach, lean):
    if number_of == 2:
        one = jax.random.randint(own_key, (), max(1, total - reach), min(reach, total - 1) + 1)
        return jnp.stack([one, total - one])
    sizes = jnp.asarray(profile(number_of, total, reach, lean), jnp.int32)
    couples = (number_of - 1) // 2
    source_of, taker = sizes[1:1 + 2 * couples:2], sizes[2:2 + 2 * couples:2]
    margin = jnp.minimum(source_of - 1, reach - taker)
    moved = jax.random.randint(jax.random.fold_in(own_key, 1), (couples,), 0, 1 << 20) % (margin + 1)
    sizes = sizes.at[1:1 + 2 * couples:2].set(source_of - moved).at[2:2 + 2 * couples:2].set(taker + moved)
    return sizes[jax.random.permutation(jax.random.fold_in(own_key, 2), number_of)]


def scatter_about(key, extent, scale, most, shards=(), held_as=jnp.bfloat16):
    values = jax.random.normal(key, extent, jnp.float32) * scale
    if len(shards) > 0:
        values = steps_of(key, extent, shards, -0.22, 0.18) * values
    return jnp.clip(values, min=-most, max=most).astype(held_as)


def setup_inputs(seed: int = 0) -> dict:
    keys = jax.random.split(jax.random.key(seed), 11)
    return {
        "latents": scatter_about(keys[0], (PATCHES, D), 1.0, 6.0, ((0, 4),)),
        "patch_route": jax.random.permutation(keys[1], PATCHES).astype(jnp.int32),
        "request_len": ragged(keys[2], REQS, PATCHES, MOST, 2).astype(jnp.int32),
        "span_order": jax.random.permutation(keys[3], SPANS).astype(jnp.int32),
        "modulation": scatter_about(keys[4], (SECTIONS, REQS, 3, D), 0.7, 4.0, ((0, 8),), jnp.float32),
        "w_qkv": scatter_about(keys[5], (SECTIONS, D, HEADS, 3 * HD), D ** -0.5, 0.109375, ((0, 8), (2, 4))),
        "w_mlp_in": scatter_about(keys[6], (SECTIONS, D, MLP), D ** -0.5, 0.109375, ((0, 8), (2, 4))),
        "w_out_attn": scatter_about(keys[7], (SECTIONS, HEADS, HD, D), (HEADS * HD + MLP) ** -0.5, 0.0625, ((0, 8), (1, 4))),
        "w_out_mlp": scatter_about(keys[8], (SECTIONS, MLP, D), (HEADS * HD + MLP) ** -0.5, 0.0625, ((0, 8), (1, 4))),
        "stale_kv": draw_stale_kv(jax.random.fold_in(keys[10], 71), 0),
    }


def layer_norm(values):
    row_mean = lax.optimization_barrier(jnp.mean(values, axis=-1, keepdims=True))
    centered = values - row_mean
    row_var = lax.optimization_barrier(jnp.mean(centered * centered, axis=-1, keepdims=True))
    return centered * lax.rsqrt(row_var + 1e-06)

def gelu_tanh(values):
    return 0.5 * values * (1.0 + jnp.tanh(0.7978845608028654 * (values + 0.044715 * values * values * values)))

def reference(latents, patch_route, request_len, span_order, modulation, w_qkv, w_mlp_in, w_out_attn, w_out_mlp, stale_kv):
    span_rows = PATCHES // SPANS
    heads_dev = HEADS // N_REQ
    mlp_dev = MLP // N_REQ
    starts = jnp.cumsum(request_len) - request_len
    patch_ids = jnp.arange(PATCHES, dtype=jnp.int32)
    owner_req = lax.optimization_barrier(jnp.sum((patch_ids[:, None] >= starts[None, :]).astype(jnp.int32), axis=1)) - 1
    seq_req = owner_req[patch_route]
    hidden = latents[patch_route]
    req_ids = jnp.arange(REQS, dtype=jnp.int32)
    for section_num in range(SECTIONS):
        mod_table = modulation[section_num].reshape(REQS, 3 * D)
        qkv_weight = w_qkv[section_num].reshape(D, HEADS * 3 * HD)
        mlp_weight = w_mlp_in[section_num]
        attn_out_weight = w_out_attn[section_num].reshape(N_REQ, heads_dev * HD, D).astype(jnp.float32)
        mlp_out_weight = w_out_mlp[section_num].reshape(N_REQ, mlp_dev, D).astype(jnp.float32)

        def block_step(carry, span_id):
            hidden_now, kv_cache = carry
            first_row = (span_id * span_rows).astype(jnp.int32)
            current = lax.dynamic_slice_in_dim(hidden_now, first_row, span_rows, 0)
            row_req = lax.dynamic_slice_in_dim(seq_req, first_row, span_rows, 0)
            onehot = (row_req[:, None] == req_ids[None, :]).astype(jnp.float32)
            mod_rows = jnp.dot(onehot, mod_table, precision=lax.Precision.HIGHEST).reshape(span_rows, 3, D)
            normed = (layer_norm(current.astype(jnp.float32)) * (1.0 + mod_rows[:, 1]) + mod_rows[:, 0]).astype(jnp.bfloat16)
            qkv_rows = jnp.dot(normed, qkv_weight, preferred_element_type=jnp.float32).reshape(span_rows, HEADS, 3 * HD)
            query_rows = qkv_rows[:, :, :HD].astype(jnp.bfloat16)
            fresh_kv = qkv_rows[:, :, HD:].astype(jnp.bfloat16)
            kv_cache = lax.dynamic_update_slice_in_dim(kv_cache, fresh_kv, first_row, 0)
            key_rows = kv_cache[:, :, :HD].astype(jnp.float32)
            value_rows = kv_cache[:, :, HD:].astype(jnp.float32)
            scores = jnp.einsum('chd,phd->hcp', query_rows.astype(jnp.float32), key_rows) / jnp.sqrt(jnp.float32(HD))
            same_req = row_req[:, None] == seq_req[None, :]
            scores = jnp.where(same_req[None], scores, -jnp.inf)
            row_top = lax.optimization_barrier(jnp.max(scores, axis=-1, keepdims=True))
            weights = jnp.exp(scores - row_top)
            weight_sum = lax.optimization_barrier(jnp.sum(weights, axis=-1, keepdims=True))
            attention = (weights / weight_sum).astype(jnp.bfloat16)
            attended = jnp.einsum('hcp,phd->chd', attention.astype(jnp.float32), value_rows).astype(jnp.bfloat16)
            mlp_act = gelu_tanh(jnp.dot(normed, mlp_weight, preferred_element_type=jnp.float32)).astype(jnp.bfloat16)
            partial_value = jnp.einsum('crk,rkd->rcd', attended.reshape(span_rows, N_REQ, heads_dev * HD).astype(jnp.float32), attn_out_weight)
            partial_value = partial_value + jnp.einsum('crk,rkd->rcd', mlp_act.reshape(span_rows, N_REQ, mlp_dev).astype(jnp.float32), mlp_out_weight)
            rounded = lax.optimization_barrier(partial_value.astype(jnp.bfloat16))
            branch = lax.optimization_barrier(jnp.sum(rounded.astype(jnp.float32), axis=0))
            updated = (current.astype(jnp.float32) + mod_rows[:, 2] * branch).astype(jnp.bfloat16)
            hidden_now = lax.dynamic_update_slice_in_dim(hidden_now, updated, first_row, 0)
            return ((hidden_now, kv_cache), jnp.int32(0))
        (hidden, last_cache), unused = lax.scan(block_step, (hidden, stale_kv[section_num]), span_order)
    return jnp.zeros_like(latents).at[patch_route].set(hidden)
```

```python
import functools

import jax
import jax.numpy as jnp
from jax import lax
from jax.experimental import pallas as pl
from jax.experimental.pallas import tpu as pltpu
from jax.sharding import PartitionSpec as P


def from_behind(block, axis, distance):
    devices = range(lax.axis_size(axis))
    route = [(i - distance, i) for i in devices if i - distance in devices]
    return lax.ppermute(block, axis, route)


def spread_2(value, axis, source):
    kept = jnp.where(lax.axis_index(axis) == source, value, 0).astype(value.dtype)
    return lax.psum(kept, axis)


def layer_norm(values):
    row_mean = jnp.mean(values, axis=-1, keepdims=True)
    centered = values - row_mean
    row_var = jnp.mean(centered * centered, axis=-1, keepdims=True)
    return centered * lax.rsqrt(row_var + 1e-06)


def gelu_tanh(values):
    return (
        0.5
        * values
        * (1.0 + jnp.tanh(0.7978845608028654 * (values + 0.044715 * values * values * values)))
    )


def plain_shards(
    latents,
    patch_route,
    request_len,
    span_order,
    modulation,
    w_qkv,
    w_mlp_in,
    w_out_attn,
    w_out_mlp,
    stale_kv,
):
    section_count = lax.axis_size("section")
    req_count = lax.axis_size("req")
    section_index = lax.axis_index("section")
    req_index = lax.axis_index("req")
    patches = patch_route.shape[0]
    span_count = span_order.shape[0]
    span_rows = patches // span_count
    model_width = latents.shape[1]
    col_width = model_width // req_count
    section_cols = model_width // section_count
    req_total = request_len.shape[0]
    heads_dev = w_qkv.shape[2]
    head_dim = w_qkv.shape[3] // 3
    starts = jnp.cumsum(request_len) - request_len
    patch_ids = jnp.arange(patches, dtype=jnp.int32)
    owner_req = jnp.sum((patch_ids[:, None] >= starts[None, :]).astype(jnp.int32), axis=1) - 1
    seq_req = owner_req[patch_route]
    req_ids = jnp.arange(req_total, dtype=jnp.int32)
    mod_table = modulation[0].reshape(req_total, 3 * model_width)
    qkv_weight = w_qkv[0].reshape(model_width, heads_dev * 3 * head_dim)
    mlp_weight = w_mlp_in[0]
    attn_out_weight = w_out_attn[0].reshape(heads_dev * head_dim, model_width)
    mlp_out_weight = w_out_mlp[0]
    spread = lax.all_to_all(latents, "req", split_axis=1, concat_axis=0, tiled=True)
    sequence = spread[patch_route]
    in_width = sequence.shape[1]

    def work(incoming, kv_cache, span_id):
        first_row = span_id * span_rows
        row_req = lax.dynamic_slice_in_dim(seq_req, first_row, span_rows, 0)
        onehot = (row_req[:, None] == req_ids[None, :]).astype(jnp.float32)
        mod_rows = jnp.dot(onehot, mod_table, precision=lax.Precision.HIGHEST).reshape(
            span_rows, 3, model_width
        )
        current = lax.all_gather(incoming, "req", axis=1, tiled=True)
        normed = (
            layer_norm(current.astype(jnp.float32)) * (1.0 + mod_rows[:, 1]) + mod_rows[:, 0]
        ).astype(jnp.bfloat16)
        qkv_rows = jnp.dot(normed, qkv_weight, preferred_element_type=jnp.float32).reshape(
            span_rows, heads_dev, 3 * head_dim
        )
        query_rows = qkv_rows[:, :, :head_dim].astype(jnp.bfloat16)
        fresh_kv = qkv_rows[:, :, head_dim:].astype(jnp.bfloat16)
        kv_cache = lax.dynamic_update_slice_in_dim(kv_cache, fresh_kv, first_row, 0)
        key_rows = kv_cache[:, :, :head_dim]
        value_rows = kv_cache[:, :, head_dim:]
        scores = jnp.einsum(
            "chd,phd->hcp", query_rows, key_rows, preferred_element_type=jnp.float32
        ) / jnp.sqrt(jnp.float32(head_dim))
        same_req = row_req[:, None] == seq_req[None, :]
        scores = jnp.where(same_req[None], scores, -jnp.inf)
        row_top = jnp.max(scores, axis=-1, keepdims=True)
        weights = jnp.exp(scores - row_top)
        weight_sum = jnp.sum(weights, axis=-1, keepdims=True)
        attention = (weights / weight_sum).astype(jnp.bfloat16)
        attended = jnp.einsum(
            "hcp,phd->chd", attention, value_rows, preferred_element_type=jnp.float32
        ).astype(jnp.bfloat16)
        attended = attended.reshape(span_rows, heads_dev * head_dim)
        mlp_act = gelu_tanh(jnp.dot(normed, mlp_weight, preferred_element_type=jnp.float32)).astype(
            jnp.bfloat16
        )
        partial_value = jnp.dot(attended, attn_out_weight, preferred_element_type=jnp.float32)
        partial_value = partial_value + jnp.dot(
            mlp_act, mlp_out_weight, preferred_element_type=jnp.float32
        )
        branch = lax.psum_scatter(
            partial_value.astype(jnp.bfloat16), "req", scatter_dimension=1, tiled=True
        ).astype(jnp.float32)
        gate_cols = lax.dynamic_slice_in_dim(mod_rows[:, 2], req_index * col_width, col_width, 1)
        updated = (incoming.astype(jnp.float32) + gate_cols * branch).astype(jnp.bfloat16)
        return (updated, kv_cache)

    def advance(moment, carry):
        incoming, kv_cache, results = carry
        span_slot = moment - section_index
        active = (span_slot >= 0) & (span_slot < span_count)
        span_id = span_order[jnp.clip(span_slot, 0, span_count - 1)]
        first_row = span_id * span_rows
        entering = lax.dynamic_slice_in_dim(sequence, first_row, span_rows, 0)
        source = jnp.where(section_index == 0, entering, incoming)
        computed, new_cache = work(source, kv_cache, span_id)
        updated = jnp.where(active, computed, jnp.zeros_like(computed))
        kv_cache = jnp.where(active, new_cache, kv_cache)
        store_here = active & (section_index == section_count - 1)
        current = lax.dynamic_slice_in_dim(results, first_row, span_rows, 0)
        results = lax.dynamic_update_slice_in_dim(
            results, jnp.where(store_here, updated, current), first_row, 0
        )
        incoming = from_behind(updated, "section", 1)
        return (incoming, kv_cache, results)

    start_state = (
        jnp.zeros((span_rows, in_width), jnp.bfloat16),
        stale_kv[0],
        jnp.zeros((patches, in_width), jnp.bfloat16),
    )
    last_in, last_cache, results = lax.fori_loop(
        0, span_count + section_count - 1, advance, start_state
    )
    finished = spread_2(results, "section", section_count - 1)
    inverse = jnp.zeros((patches,), jnp.int32).at[patch_route].set(patch_ids)
    unrouted = finished[inverse]
    owned = lax.all_to_all(unrouted, "req", split_axis=0, concat_axis=1, tiled=True)
    return lax.dynamic_slice_in_dim(owned, section_index * section_cols, section_cols, 1)


MESH = pl.DeviceIdType.MESH
F32 = jnp.float32
BF16 = jnp.bfloat16


def dot(left, right, dims=((1,), (0,)), precision=None):
    return lax.dot_general(
        left, right, (dims, ((), ())), precision=precision, preferred_element_type=F32
    )


def relay_kernel(
    sections,
    reqs,
    route_ref,
    len_ref,
    order_ref,
    latents_ref,
    mod_ref,
    stale_ref,
    w_qkv_ref,
    w_in_ref,
    w_attn_ref,
    w_mlp_ref,
    out_ref,
    wq,
    wi,
    wo,
    lat,
    xin,
    normed,
    act,
    kv,
    same,
    perm,
    mods,
    part_send,
    part_recv,
    xnew,
    xfin,
    fin_send,
    fin_recv,
    w_sem,
    lat_ssem,
    lat_rsem,
    x_ssem,
    x_rsem,
    p_ssem,
    p_rsem,
    f_ssem,
    f_rsem,
):
    s = lax.axis_index("section")
    r = lax.axis_index("req")
    devices = sections * reqs
    per = sections // reqs
    patches, width = lat.shape
    rows = patches // 2
    cols = width // reqs
    own_rows = patches // reqs
    heads, _, head_width = wq.shape
    hd = head_width // 3
    attn_width = heads * hd
    mlp_width = wi.shape[1]
    req_total = mod_ref.shape[1]

    loads = [
        pltpu.make_async_copy(w_qkv_ref, wq, w_sem.at[0]),
        pltpu.make_async_copy(w_in_ref, wi, w_sem.at[1]),
        pltpu.make_async_copy(w_attn_ref, wo.at[pl.ds(0, attn_width)], w_sem.at[2]),
        pltpu.make_async_copy(w_mlp_ref, wo.at[pl.ds(attn_width, mlp_width)], w_sem.at[3]),
    ]
    for load in loads:
        load.start()

    barrier = pltpu.get_barrier_semaphore()
    me = s * reqs + r

    def greet(step, carry):
        target = lax.rem(me + step, devices)
        pl.semaphore_signal(
            barrier,
            inc=1,
            device_id=(lax.div(target, reqs), lax.rem(target, reqs)),
            device_id_type=MESH,
        )
        return carry

    lax.fori_loop(1, devices, greet, 0)
    pl.semaphore_wait(barrier, devices - 1)

    def peer(step):
        return lax.rem(r + step, reqs)

    def lat_copy(step):
        mine = lat.at[pl.ds(pl.multiple_of(r * own_rows, own_rows), own_rows)]
        return pltpu.make_async_remote_copy(
            src_ref=latents_ref,
            dst_ref=mine,
            send_sem=lat_ssem.at[step],
            recv_sem=lat_rsem.at[step],
            device_id=(s, peer(step)),
            device_id_type=MESH,
        )

    @pl.when(s == 0)
    def _():
        for step in range(1, reqs):
            lat_copy(step).start()
        lat[pl.ds(pl.multiple_of(r * own_rows, own_rows), own_rows), :] = latents_ref[...]

    place = lax.broadcasted_iota(jnp.int32, (patches, patches), 0)
    lane = lax.broadcasted_iota(jnp.int32, (patches, patches), 1)
    first, second = order_ref[0], order_ref[1]
    position = jnp.where(place < rows, first * rows + place, second * rows + place - rows)
    chosen = lane == position
    route = jnp.sum(
        jnp.where(chosen, jnp.broadcast_to(route_ref[...], chosen.shape), 0).astype(F32),
        axis=1,
        keepdims=True,
    )
    perm[...] = (lane.astype(F32) == route).astype(BF16)
    req_lane = lax.broadcasted_iota(jnp.int32, (patches, req_total), 1)
    owner = jnp.zeros((patches, req_total), F32)
    start = jnp.int32(0)
    for q in range(req_total):
        end = start + len_ref[q]
        inside = (route >= start.astype(F32)) & (route < end.astype(F32))
        owner = jnp.where((req_lane == q) & inside, 1.0, owner)
        start = end
    same[...] = dot(owner, owner, ((1,), (1,)))
    chosen_bf = chosen.astype(F32).astype(BF16)
    for h in range(heads):
        kv[h, rows:, :] = dot(chosen_bf[rows:, :], stale_ref[h]).astype(BF16)
    for k in range(3):
        for c in range(reqs):
            at = pl.ds(c * cols, cols)
            value = dot(owner, mod_ref[k, :, at], precision=lax.Precision.HIGHEST)
            mods[k, :, at] = value + 1.0 if k == 1 else value

    @pl.when(s == 0)
    def _():
        for step in range(1, reqs):
            lat_copy(step).wait_recv()
        for c in range(reqs):
            entry = dot(perm[...], lat[:, c * cols : (c + 1) * cols]).astype(BF16)
            xin[0, c] = entry[:rows]
            xin[1, c] = entry[rows:]

    def x_copy(t, q, source):
        return pltpu.make_async_remote_copy(
            src_ref=xnew.at[t],
            dst_ref=xin.at[t, source],
            send_sem=x_ssem.at[t, q],
            recv_sem=x_rsem.at[t, source],
            device_id=(lax.rem(s + 1, sections), q),
            device_id_type=MESH,
        )

    def part_copy(t, step):
        return pltpu.make_async_remote_copy(
            src_ref=part_send.at[t, step],
            dst_ref=part_recv.at[t, step],
            send_sem=p_ssem.at[t, step],
            recv_sem=p_rsem.at[t, step],
            device_id=(s, peer(step)),
            device_id_type=MESH,
        )

    def slot(t, carry):
        at_rows = pl.ds(pl.multiple_of(t * rows, rows), rows)

        @pl.when(s > 0)
        def _():
            for q in range(reqs):
                x_copy(t, q, q).wait_recv()

        total = jnp.zeros((rows, 1), F32)
        for c in range(reqs):
            total = total + jnp.sum(xin[t, c].astype(F32), axis=1, keepdims=True)
        mean = total / width
        square = jnp.zeros((rows, 1), F32)
        for c in range(reqs):
            centered = xin[t, c].astype(F32) - mean
            square = square + jnp.sum(centered * centered, axis=1, keepdims=True)
        scale = lax.rsqrt(square / width + 1e-06)
        for c in range(reqs):
            at = pl.ds(c * cols, cols)
            value = (xin[t, c].astype(F32) - mean) * scale
            normed[:, at] = (value * mods[1, at_rows, at] + mods[0, at_rows, at]).astype(BF16)

        @pl.when(t == 0)
        def _():
            loads[0].wait()

        allowed = same[at_rows, :] > 0.5
        for h in range(heads):
            qkv = dot(normed[...], wq[h])
            kv[h, at_rows, :] = qkv[:, hd:].astype(BF16)
            scores = dot(qkv[:, :hd].astype(BF16), kv[h, :, :hd], ((1,), (1,))) * (hd**-0.5)
            scores = jnp.where(allowed, scores, -jnp.inf)
            top = jnp.max(scores, axis=1, keepdims=True)
            weights = jnp.exp(scores - top)
            weights = weights / jnp.sum(weights, axis=1, keepdims=True)
            act[:, h * hd : (h + 1) * hd] = dot(weights.astype(BF16), kv[h, :, hd:]).astype(BF16)

        @pl.when(t == 0)
        def _():
            loads[1].wait()

        piece = mlp_width // 3 if mlp_width % 384 == 0 else mlp_width
        for c in range(mlp_width // piece):
            hidden = dot(normed[...], wi[:, c * piece : (c + 1) * piece])
            act[:, attn_width + c * piece : attn_width + (c + 1) * piece] = gelu_tanh(
                hidden
            ).astype(BF16)

        @pl.when(t == 0)
        def _():
            loads[2].wait()
            loads[3].wait()

        for step in [*range(reqs - 1, 0, -1), 0]:
            at = pl.ds(pl.multiple_of(peer(step) * cols, cols), cols)
            part_send[t, step] = dot(act[...], wo[:, at]).astype(BF16)
            if step > 0:
                part_copy(t, step).start()
        branch = part_send[t, 0].astype(F32)
        for step in range(reqs - 1, 0, -1):
            part_copy(t, step).wait_recv()
            branch = branch + part_recv[t, step].astype(F32)
        own = pl.ds(pl.multiple_of(r * cols, cols), cols)
        gated = mods[2, at_rows, own] * branch
        updated = (xin[t, r].astype(F32) + gated).astype(BF16)
        xnew[t] = updated

        @pl.when(s < sections - 1)
        def _():
            for q in range(reqs):
                x_copy(t, q, r).start()

        @pl.when(s == sections - 1)
        def _():
            xfin[at_rows, :] = updated

        return carry

    lax.fori_loop(0, 2, slot, 0)

    last_own = (sections - 1) // per
    is_self = (s == sections - 1) & (r == last_own)

    def fin_copy(u, q):
        return pltpu.make_async_remote_copy(
            src_ref=fin_send.at[u, q],
            dst_ref=fin_recv,
            send_sem=f_ssem.at[u, q],
            recv_sem=f_rsem.at[0],
            device_id=(r * per + u, q),
            device_id_type=MESH,
        )

    def to_self(u, q):
        return (r * per + u == sections - 1) & (r == q)

    @pl.when(s == sections - 1)
    def _():
        done = dot(perm[...], xfin[...], ((0,), (0,))).astype(BF16)
        out_cols = cols // per
        for u in range(per):
            for q in range(reqs):
                block = done[q * own_rows : (q + 1) * own_rows, u * out_cols : (u + 1) * out_cols]
                fin_send[u, q] = block

                @pl.when(to_self(u, q))
                def _():
                    out_ref[...] = block

                @pl.when(jnp.logical_not(to_self(u, q)))
                def _():
                    fin_copy(u, q).start()

    @pl.when(jnp.logical_not(is_self))
    def _():
        fin_copy(0, 0).wait_recv()
        out_ref[...] = fin_recv[...]

    @pl.when(s == sections - 1)
    def _():
        for u in range(per):
            for q in range(reqs):

                @pl.when(jnp.logical_not(to_self(u, q)))
                def _():
                    fin_copy(u, q).wait_send()

    @pl.when(s == 0)
    def _():
        for step in range(1, reqs):
            lat_copy(step).wait_send()

    for t in range(2):
        for step in range(1, reqs):
            part_copy(t, step).wait_send()

    @pl.when(s < sections - 1)
    def _():
        for t in range(2):
            for q in range(reqs):
                x_copy(t, q, r).wait_send()


def relay_shards(
    latents,
    patch_route,
    request_len,
    span_order,
    modulation,
    w_qkv,
    w_mlp_in,
    w_out_attn,
    w_out_mlp,
    stale_kv,
):
    sections = lax.axis_size("section")
    reqs = lax.axis_size("req")
    patches = patch_route.shape[0]
    own_rows, width = latents.shape
    heads, head_width = w_qkv.shape[2:]
    hd = head_width // 3
    mlp_width = w_mlp_in.shape[2]
    rows, cols, per = patches // 2, width // reqs, sections // reqs
    out_cols = width // sections
    vmem = pl.BlockSpec(memory_space=pltpu.VMEM)
    smem = pl.BlockSpec(memory_space=pltpu.SMEM)
    hbm = pl.BlockSpec(memory_space=pl.ANY)
    weights = width * (heads * head_width + mlp_width) + (heads * hd + mlp_width) * width
    return pl.pallas_call(
        functools.partial(relay_kernel, sections, reqs),
        out_shape=jax.ShapeDtypeStruct((own_rows, out_cols), BF16),
        in_specs=[vmem, smem, smem, vmem, vmem, vmem, hbm, hbm, hbm, hbm],
        out_specs=vmem,
        scratch_shapes=[
            pltpu.VMEM((heads, width, head_width), BF16),
            pltpu.VMEM((width, mlp_width), BF16),
            pltpu.VMEM((heads * hd + mlp_width, width), BF16),
            pltpu.VMEM((patches, width), BF16),
            pltpu.VMEM((2, reqs, rows, cols), BF16),
            pltpu.VMEM((rows, width), BF16),
            pltpu.VMEM((rows, heads * hd + mlp_width), BF16),
            pltpu.VMEM((heads, patches, 2 * hd), BF16),
            pltpu.VMEM((patches, patches), F32),
            pltpu.VMEM((patches, patches), BF16),
            pltpu.VMEM((3, patches, width), F32),
            pltpu.VMEM((2, reqs, rows, cols), BF16),
            pltpu.VMEM((2, reqs, rows, cols), BF16),
            pltpu.VMEM((2, rows, cols), BF16),
            pltpu.VMEM((patches, cols), BF16),
            pltpu.VMEM((per, reqs, own_rows, out_cols), BF16),
            pltpu.VMEM((own_rows, out_cols), BF16),
            pltpu.SemaphoreType.DMA((4,)),
            pltpu.SemaphoreType.DMA((reqs,)),
            pltpu.SemaphoreType.DMA((reqs,)),
            pltpu.SemaphoreType.DMA((2, reqs)),
            pltpu.SemaphoreType.DMA((2, reqs)),
            pltpu.SemaphoreType.DMA((2, reqs)),
            pltpu.SemaphoreType.DMA((2, reqs)),
            pltpu.SemaphoreType.DMA((per, reqs)),
            pltpu.SemaphoreType.DMA((1,)),
        ],
        compiler_params=pltpu.CompilerParams(
            collective_id=0, has_side_effects=True, vmem_limit_bytes=58 * 2**20
        ),
        cost_estimate=pl.CostEstimate(
            flops=2 * patches * weights, bytes_accessed=2 * weights, transcendentals=0
        ),
    )(
        patch_route.reshape(1, patches),
        request_len,
        span_order,
        latents,
        jnp.transpose(modulation[0], (1, 0, 2)),
        jnp.transpose(stale_kv[0], (1, 0, 2)),
        jnp.transpose(w_qkv[0], (1, 0, 2)),
        w_mlp_in[0],
        w_out_attn[0].reshape(heads * hd, width),
        w_out_mlp[0],
    )


def shards(*arrays):
    sections, reqs = lax.axis_size("section"), lax.axis_size("req")
    width, patches = arrays[0].shape[1], arrays[1].shape[0]
    fits = (
        arrays[3].shape[0] == 2
        and sections % reqs == 0
        and width % (sections * 128) == 0
        and patches % (reqs * 16) == 0
    )
    return (relay_shards if fits else plain_shards)(*arrays)


def solution(mesh):
    in_specs = (
        P("req", None),
        P(),
        P(),
        P(),
        P("section", None, None, None),
        P("section", None, "req", None),
        P("section", None, "req"),
        P("section", "req", None, None),
        P("section", "req", None),
        P("section", None, "req", None),
    )
    out_specs = P("req", "section")
    return jax.shard_map(shards, mesh=mesh, in_specs=in_specs, out_specs=out_specs, check_vma=False)
```

```python
import functools

import jax
import jax.numpy as jnp
from jax import lax
from jax.experimental import pallas as pl
from jax.experimental.pallas import tpu as pltpu
from jax.sharding import PartitionSpec as P


def from_behind(block, axis, distance):
    devices = range(lax.axis_size(axis))
    route = [(i - distance, i) for i in devices if i - distance in devices]
    return lax.ppermute(block, axis, route)


def spread_2(value, axis, source):
    kept = jnp.where(lax.axis_index(axis) == source, value, 0).astype(value.dtype)
    return lax.psum(kept, axis)


def layer_norm(values):
    row_mean = jnp.mean(values, axis=-1, keepdims=True)
    centered = values - row_mean
    row_var = jnp.mean(centered * centered, axis=-1, keepdims=True)
    return centered * lax.rsqrt(row_var + 1e-06)


def gelu_tanh(values):
    return (
        0.5
        * values
        * (1.0 + jnp.tanh(0.7978845608028654 * (values + 0.044715 * values * values * values)))
    )


def plain_shards(
    latents,
    patch_route,
    request_len,
    span_order,
    modulation,
    w_qkv,
    w_mlp_in,
    w_out_attn,
    w_out_mlp,
    stale_kv,
):
    section_count = lax.axis_size("section")
    req_count = lax.axis_size("req")
    section_index = lax.axis_index("section")
    req_index = lax.axis_index("req")
    patches = patch_route.shape[0]
    span_count = span_order.shape[0]
    span_rows = patches // span_count
    model_width = latents.shape[1]
    col_width = model_width // req_count
    section_cols = model_width // section_count
    req_total = request_len.shape[0]
    heads_dev = w_qkv.shape[2]
    head_dim = w_qkv.shape[3] // 3
    starts = jnp.cumsum(request_len) - request_len
    patch_ids = jnp.arange(patches, dtype=jnp.int32)
    owner_req = jnp.sum((patch_ids[:, None] >= starts[None, :]).astype(jnp.int32), axis=1) - 1
    seq_req = owner_req[patch_route]
    req_ids = jnp.arange(req_total, dtype=jnp.int32)
    mod_table = modulation[0].reshape(req_total, 3 * model_width)
    qkv_weight = w_qkv[0].reshape(model_width, heads_dev * 3 * head_dim)
    mlp_weight = w_mlp_in[0]
    attn_out_weight = w_out_attn[0].reshape(heads_dev * head_dim, model_width)
    mlp_out_weight = w_out_mlp[0]
    spread = lax.all_to_all(latents, "req", split_axis=1, concat_axis=0, tiled=True)
    sequence = spread[patch_route]
    in_width = sequence.shape[1]

    def work(incoming, kv_cache, span_id):
        first_row = span_id * span_rows
        row_req = lax.dynamic_slice_in_dim(seq_req, first_row, span_rows, 0)
        onehot = (row_req[:, None] == req_ids[None, :]).astype(jnp.float32)
        mod_rows = jnp.dot(onehot, mod_table, precision=lax.Precision.HIGHEST).reshape(
            span_rows, 3, model_width
        )
        current = lax.all_gather(incoming, "req", axis=1, tiled=True)
        normed = (
            layer_norm(current.astype(jnp.float32)) * (1.0 + mod_rows[:, 1]) + mod_rows[:, 0]
        ).astype(jnp.bfloat16)
        qkv_rows = jnp.dot(normed, qkv_weight, preferred_element_type=jnp.float32).reshape(
            span_rows, heads_dev, 3 * head_dim
        )
        query_rows = qkv_rows[:, :, :head_dim].astype(jnp.bfloat16)
        fresh_kv = qkv_rows[:, :, head_dim:].astype(jnp.bfloat16)
        kv_cache = lax.dynamic_update_slice_in_dim(kv_cache, fresh_kv, first_row, 0)
        key_rows = kv_cache[:, :, :head_dim]
        value_rows = kv_cache[:, :, head_dim:]
        scores = jnp.einsum(
            "chd,phd->hcp", query_rows, key_rows, preferred_element_type=jnp.float32
        ) / jnp.sqrt(jnp.float32(head_dim))
        same_req = row_req[:, None] == seq_req[None, :]
        scores = jnp.where(same_req[None], scores, -jnp.inf)
        row_top = jnp.max(scores, axis=-1, keepdims=True)
        weights = jnp.exp(scores - row_top)
        weight_sum = jnp.sum(weights, axis=-1, keepdims=True)
        attention = (weights / weight_sum).astype(jnp.bfloat16)
        attended = jnp.einsum(
            "hcp,phd->chd", attention, value_rows, preferred_element_type=jnp.float32
        ).astype(jnp.bfloat16)
        attended = attended.reshape(span_rows, heads_dev * head_dim)
        mlp_act = gelu_tanh(jnp.dot(normed, mlp_weight, preferred_element_type=jnp.float32)).astype(
            jnp.bfloat16
        )
        partial_value = jnp.dot(attended, attn_out_weight, preferred_element_type=jnp.float32)
        partial_value = partial_value + jnp.dot(
            mlp_act, mlp_out_weight, preferred_element_type=jnp.float32
        )
        branch = lax.psum_scatter(
            partial_value.astype(jnp.bfloat16), "req", scatter_dimension=1, tiled=True
        ).astype(jnp.float32)
        gate_cols = lax.dynamic_slice_in_dim(mod_rows[:, 2], req_index * col_width, col_width, 1)
        updated = (incoming.astype(jnp.float32) + gate_cols * branch).astype(jnp.bfloat16)
        return (updated, kv_cache)

    def advance(moment, carry):
        incoming, kv_cache, results = carry
        span_slot = moment - section_index
        active = (span_slot >= 0) & (span_slot < span_count)
        span_id = span_order[jnp.clip(span_slot, 0, span_count - 1)]
        first_row = span_id * span_rows
        entering = lax.dynamic_slice_in_dim(sequence, first_row, span_rows, 0)
        source = jnp.where(section_index == 0, entering, incoming)
        computed, new_cache = work(source, kv_cache, span_id)
        updated = jnp.where(active, computed, jnp.zeros_like(computed))
        kv_cache = jnp.where(active, new_cache, kv_cache)
        store_here = active & (section_index == section_count - 1)
        current = lax.dynamic_slice_in_dim(results, first_row, span_rows, 0)
        results = lax.dynamic_update_slice_in_dim(
            results, jnp.where(store_here, updated, current), first_row, 0
        )
        incoming = from_behind(updated, "section", 1)
        return (incoming, kv_cache, results)

    start_state = (
        jnp.zeros((span_rows, in_width), jnp.bfloat16),
        stale_kv[0],
        jnp.zeros((patches, in_width), jnp.bfloat16),
    )
    last_in, last_cache, results = lax.fori_loop(
        0, span_count + section_count - 1, advance, start_state
    )
    finished = spread_2(results, "section", section_count - 1)
    inverse = jnp.zeros((patches,), jnp.int32).at[patch_route].set(patch_ids)
    unrouted = finished[inverse]
    owned = lax.all_to_all(unrouted, "req", split_axis=0, concat_axis=1, tiled=True)
    return lax.dynamic_slice_in_dim(owned, section_index * section_cols, section_cols, 1)


MESH = pl.DeviceIdType.MESH
F32 = jnp.float32
BF16 = jnp.bfloat16


def dot(left, right, dims=((1,), (0,)), precision=None):
    return lax.dot_general(
        left, right, (dims, ((), ())), precision=precision, preferred_element_type=F32
    )


def relay_kernel(
    sections,
    reqs,
    route_ref,
    len_ref,
    order_ref,
    latents_ref,
    mod_ref,
    stale_ref,
    w_qkv_ref,
    w_in_ref,
    w_attn_ref,
    w_mlp_ref,
    out_ref,
    wq,
    wi,
    wo,
    lat,
    xin,
    normed,
    act,
    kv,
    same,
    perm,
    mods,
    part_send,
    part_recv,
    xnew,
    xfin,
    fin_send,
    fin_recv,
    w_sem,
    lat_ssem,
    lat_rsem,
    x_ssem,
    x_rsem,
    p_ssem,
    p_rsem,
    f_ssem,
    f_rsem,
):
    s = lax.axis_index("section")
    r = lax.axis_index("req")
    devices = sections * reqs
    per = sections // reqs
    patches, width = lat.shape
    rows = patches // 2
    cols = width // reqs
    own_rows = patches // reqs
    heads, _, head_width = w_qkv_ref.shape
    hd = head_width // 3
    pieces = [(0, cols)] if cols < 512 else [(0, cols - 256), (cols - 256, 256)]
    attn_width = heads * hd
    mlp_width = wi.shape[1]
    req_total = mod_ref.shape[1]

    loads = [
        pltpu.make_async_copy(
            w_qkv_ref.at[h], wq.at[:, pl.ds(h * head_width, head_width)], w_sem.at[3 + h]
        )
        for h in range(heads)
    ]
    loads.append(pltpu.make_async_copy(w_in_ref, wi, w_sem.at[0]))
    late_loads = [
        pltpu.make_async_copy(w_attn_ref, wo.at[pl.ds(0, attn_width)], w_sem.at[1]),
        pltpu.make_async_copy(w_mlp_ref, wo.at[pl.ds(attn_width, mlp_width)], w_sem.at[2]),
    ]
    for load in loads + late_loads:
        load.start()

    barrier = pltpu.get_barrier_semaphore()
    me = s * reqs + r

    def greet(step, carry):
        target = lax.rem(me + step, devices)
        pl.semaphore_signal(
            barrier,
            inc=1,
            device_id=(lax.div(target, reqs), lax.rem(target, reqs)),
            device_id_type=MESH,
        )
        return carry

    lax.fori_loop(1, devices, greet, 0)
    pl.semaphore_wait(barrier, devices - 1)

    def peer(step):
        if reqs % 2:
            return lax.rem(r + step, reqs)
        across = lax.rem(lax.div(r, 2) + step // 2, reqs // 2)
        return across * 2 + lax.rem(r + step, 2)

    def lat_copy(step):
        mine = lat.at[pl.ds(pl.multiple_of(r * own_rows, own_rows), own_rows)]
        return pltpu.make_async_remote_copy(
            src_ref=latents_ref,
            dst_ref=mine,
            send_sem=lat_ssem.at[step],
            recv_sem=lat_rsem.at[step],
            device_id=(s, peer(step)),
            device_id_type=MESH,
        )

    @pl.when(s == 0)
    def _():
        for step in range(1, reqs):
            lat_copy(step).start()
        lat[pl.ds(pl.multiple_of(r * own_rows, own_rows), own_rows), :] = latents_ref[...]

    place = lax.broadcasted_iota(jnp.int32, (patches, patches), 0)
    lane = lax.broadcasted_iota(jnp.int32, (patches, patches), 1)
    first, second = order_ref[0], order_ref[1]
    position = jnp.where(place < rows, first * rows + place, second * rows + place - rows)
    chosen = lane == position
    route = jnp.sum(
        jnp.where(chosen, jnp.broadcast_to(route_ref[...], chosen.shape), 0).astype(F32),
        axis=1,
        keepdims=True,
    )
    perm[...] = (lane.astype(F32) == route).astype(BF16)
    req_lane = lax.broadcasted_iota(jnp.int32, (patches, req_total), 1)
    owner = jnp.zeros((patches, req_total), F32)
    start = jnp.int32(0)
    for q in range(req_total):
        end = start + len_ref[q]
        inside = (route >= start.astype(F32)) & (route < end.astype(F32))
        owner = jnp.where((req_lane == q) & inside, 1.0, owner)
        start = end
    same[...] = dot(owner, owner, ((1,), (1,)))
    chosen_bf = chosen.astype(F32).astype(BF16)
    for h in range(heads):
        kv[h, rows:, :] = dot(chosen_bf[rows:, :], stale_ref[h]).astype(BF16)
    for k in range(3):
        for c in range(reqs):
            at = pl.ds(c * cols, cols)
            value = dot(owner, mod_ref[k, :, at], precision=lax.Precision.HIGHEST)
            mods[k, :, at] = value + 1.0 if k == 1 else value

    @pl.when(s == 0)
    def _():
        for step in range(1, reqs):
            lat_copy(step).wait_recv()
        for c in range(reqs):
            entry = dot(perm[...], lat[:, c * cols : (c + 1) * cols]).astype(BF16)
            xin[0, c] = entry[:rows]
            xin[1, c] = entry[rows:]

    def x_copy(p, t, q, source):
        at = pl.ds(*pieces[p])
        return pltpu.make_async_remote_copy(
            src_ref=xnew.at[t, :, at],
            dst_ref=xin.at[t, source, :, at],
            send_sem=x_ssem.at[p, t, q],
            recv_sem=x_rsem.at[p, t, source],
            device_id=(lax.rem(s + 1, sections), q),
            device_id_type=MESH,
        )

    def part_copy(p, t, step):
        at = pl.ds(*pieces[p])
        return pltpu.make_async_remote_copy(
            src_ref=part_send.at[t, step, :, at],
            dst_ref=part_recv.at[t, step, :, at],
            send_sem=p_ssem.at[p, t, step],
            recv_sem=p_rsem.at[p, t, step],
            device_id=(s, peer(step)),
            device_id_type=MESH,
        )

    def slot(t, carry):
        at_rows = pl.ds(pl.multiple_of(t * rows, rows), rows)

        stats = []
        for p, (begin, size) in enumerate(pieces):
            for q in range(reqs):

                @pl.when(s > 0)
                def _():
                    x_copy(p, t, q, q).wait_recv()

            for q in range(reqs):
                value = xin[t, q, :, begin : begin + size].astype(F32)
                mean = jnp.sum(value, axis=1, keepdims=True) / size
                value = value - mean
                stats.append((size, mean, jnp.sum(value * value, axis=1, keepdims=True)))
        mean = sum(size * part for size, part, _ in stats) / width
        square = sum(part + size * (at - mean) * (at - mean) for size, at, part in stats)
        scale = lax.rsqrt(square / width + 1e-06)
        for c in range(reqs):
            at = pl.ds(c * cols, cols)
            value = (xin[t, c].astype(F32) - mean) * scale
            normed[:, at] = (value * mods[1, at_rows, at] + mods[0, at_rows, at]).astype(BF16)

        @pl.when(t == 0)
        def _():
            for load in loads:
                load.wait()

        allowed = same[at_rows, :] > 0.5
        group = 2 if heads % 2 == 0 else 1
        queries = []
        for g in range(heads // group):
            span = group * head_width
            qkv = dot(normed[...], wq[:, g * span : (g + 1) * span])
            for h in range(group):
                begin = h * head_width
                queries.append(qkv[:, begin : begin + hd].astype(BF16))
                fresh = qkv[:, begin + hd : begin + head_width].astype(BF16)
                kv[g * group + h, at_rows, :] = fresh

        piece = mlp_width // 3 if mlp_width % 384 == 0 else mlp_width
        chunks = mlp_width // piece

        def up(c):
            return dot(normed[...], wi[:, c * piece : (c + 1) * piece])

        def keep(c, hidden):
            at = attn_width + c * piece
            act[:, at : at + piece] = gelu_tanh(hidden).astype(BF16)

        scores = [dot(queries[h], kv[h, :, :hd], ((1,), (1,))) for h in range(heads)]
        hidden = up(0)
        attention = []
        for h in range(heads):
            score = jnp.where(allowed, scores[h] * (hd**-0.5), -jnp.inf)
            top = jnp.max(score, axis=1, keepdims=True)
            weights = jnp.exp(score - top)
            weights = weights / jnp.sum(weights, axis=1, keepdims=True)
            attention.append(weights.astype(BF16))
        keep(0, hidden)
        for c in range(1, chunks):
            hidden = up(c)
            if c == 1:
                for h in range(heads):
                    act[:, h * hd : (h + 1) * hd] = dot(attention[h], kv[h, :, hd:]).astype(BF16)
            keep(c, hidden)
        if chunks == 1:
            for h in range(heads):
                act[:, h * hd : (h + 1) * hd] = dot(attention[h], kv[h, :, hd:]).astype(BF16)

        @pl.when(t == 0)
        def _():
            for load in late_loads:
                load.wait()

        for p, (begin, size) in enumerate(pieces):
            for step in [*range(reqs - 1, 0, -1), 0]:
                at = pl.ds(pl.multiple_of(peer(step) * cols + begin, 128), size)
                product = dot(act[...], wo[:, at]).astype(BF16)
                part_send[t, step, :, begin : begin + size] = product
                if step > 0:
                    part_copy(p, t, step).start()
        for p, (begin, size) in enumerate(pieces):
            branch = part_send[t, 0, :, begin : begin + size].astype(F32)
            for step in range(1, reqs):
                part_copy(p, t, step).wait_recv()
                branch = branch + part_recv[t, step, :, begin : begin + size].astype(F32)
            own = pl.ds(pl.multiple_of(r * cols + begin, 128), size)
            gated = mods[2, at_rows, own] * branch
            updated = xin[t, r, :, begin : begin + size].astype(F32) + gated
            xnew[t, :, begin : begin + size] = updated.astype(BF16)

            @pl.when(s < sections - 1)
            def _():
                for step in range(reqs - 1, -1, -1):
                    x_copy(p, t, peer(step), r).start()

        @pl.when(s == sections - 1)
        def _():
            xfin[at_rows, :] = xnew[t]

        return carry

    lax.fori_loop(0, 2, slot, 0)

    last_own = (sections - 1) // per
    is_self = (s == sections - 1) & (r == last_own)

    def fin_copy(u, q):
        return pltpu.make_async_remote_copy(
            src_ref=fin_send.at[u, q],
            dst_ref=fin_recv,
            send_sem=f_ssem.at[u, q],
            recv_sem=f_rsem.at[0],
            device_id=(r * per + u, q),
            device_id_type=MESH,
        )

    def to_self(u, q):
        return (r * per + u == sections - 1) & (r == q)

    @pl.when(s == sections - 1)
    def _():
        done = dot(perm[...], xfin[...], ((0,), (0,))).astype(BF16)
        out_cols = cols // per
        for u in range(per):
            for q in range(reqs):
                block = done[q * own_rows : (q + 1) * own_rows, u * out_cols : (u + 1) * out_cols]
                fin_send[u, q] = block

                @pl.when(to_self(u, q))
                def _():
                    out_ref[...] = block

                @pl.when(jnp.logical_not(to_self(u, q)))
                def _():
                    fin_copy(u, q).start()

    @pl.when(jnp.logical_not(is_self))
    def _():
        fin_copy(0, 0).wait_recv()
        out_ref[...] = fin_recv[...]

    @pl.when(s == sections - 1)
    def _():
        for u in range(per):
            for q in range(reqs):

                @pl.when(jnp.logical_not(to_self(u, q)))
                def _():
                    fin_copy(u, q).wait_send()

    @pl.when(s == 0)
    def _():
        for step in range(1, reqs):
            lat_copy(step).wait_send()

    for p in range(len(pieces)):
        for t in range(2):
            for step in range(1, reqs):
                part_copy(p, t, step).wait_send()

    @pl.when(s < sections - 1)
    def _():
        for p in range(len(pieces)):
            for t in range(2):
                for q in range(reqs):
                    x_copy(p, t, q, r).wait_send()


def relay_shards(
    latents,
    patch_route,
    request_len,
    span_order,
    modulation,
    w_qkv,
    w_mlp_in,
    w_out_attn,
    w_out_mlp,
    stale_kv,
):
    sections = lax.axis_size("section")
    reqs = lax.axis_size("req")
    patches = patch_route.shape[0]
    own_rows, width = latents.shape
    heads, head_width = w_qkv.shape[2:]
    hd = head_width // 3
    mlp_width = w_mlp_in.shape[2]
    rows, cols, per = patches // 2, width // reqs, sections // reqs
    out_cols = width // sections
    vmem = pl.BlockSpec(memory_space=pltpu.VMEM)
    smem = pl.BlockSpec(memory_space=pltpu.SMEM)
    hbm = pl.BlockSpec(memory_space=pl.ANY)
    weights = width * (heads * head_width + mlp_width) + (heads * hd + mlp_width) * width
    return pl.pallas_call(
        functools.partial(relay_kernel, sections, reqs),
        out_shape=jax.ShapeDtypeStruct((own_rows, out_cols), BF16),
        in_specs=[vmem, smem, smem, vmem, vmem, vmem, hbm, hbm, hbm, hbm],
        out_specs=vmem,
        scratch_shapes=[
            pltpu.VMEM((width, heads * head_width), BF16),
            pltpu.VMEM((width, mlp_width), BF16),
            pltpu.VMEM((heads * hd + mlp_width, width), BF16),
            pltpu.VMEM((patches, width), BF16),
            pltpu.VMEM((2, reqs, rows, cols), BF16),
            pltpu.VMEM((rows, width), BF16),
            pltpu.VMEM((rows, heads * hd + mlp_width), BF16),
            pltpu.VMEM((heads, patches, 2 * hd), BF16),
            pltpu.VMEM((patches, patches), F32),
            pltpu.VMEM((patches, patches), BF16),
            pltpu.VMEM((3, patches, width), F32),
            pltpu.VMEM((2, reqs, rows, cols), BF16),
            pltpu.VMEM((2, reqs, rows, cols), BF16),
            pltpu.VMEM((2, rows, cols), BF16),
            pltpu.VMEM((patches, cols), BF16),
            pltpu.VMEM((per, reqs, own_rows, out_cols), BF16),
            pltpu.VMEM((own_rows, out_cols), BF16),
            pltpu.SemaphoreType.DMA((3 + heads,)),
            pltpu.SemaphoreType.DMA((reqs,)),
            pltpu.SemaphoreType.DMA((reqs,)),
            pltpu.SemaphoreType.DMA((2, 2, reqs)),
            pltpu.SemaphoreType.DMA((2, 2, reqs)),
            pltpu.SemaphoreType.DMA((2, 2, reqs)),
            pltpu.SemaphoreType.DMA((2, 2, reqs)),
            pltpu.SemaphoreType.DMA((per, reqs)),
            pltpu.SemaphoreType.DMA((1,)),
        ],
        compiler_params=pltpu.CompilerParams(
            collective_id=0, has_side_effects=True, vmem_limit_bytes=58 * 2**20
        ),
        cost_estimate=pl.CostEstimate(
            flops=2 * patches * weights, bytes_accessed=2 * weights, transcendentals=0
        ),
    )(
        patch_route.reshape(1, patches),
        request_len,
        span_order,
        latents,
        jnp.transpose(modulation[0], (1, 0, 2)),
        jnp.transpose(stale_kv[0], (1, 0, 2)),
        jnp.transpose(w_qkv[0], (1, 0, 2)),
        w_mlp_in[0],
        w_out_attn[0].reshape(heads * hd, width),
        w_out_mlp[0],
    )


def shards(*arrays):
    sections, reqs = lax.axis_size("section"), lax.axis_size("req")
    width, patches = arrays[0].shape[1], arrays[1].shape[0]
    fits = (
        arrays[3].shape[0] == 2
        and sections % reqs == 0
        and width % (sections * 128) == 0
        and patches % (reqs * 16) == 0
    )
    return (relay_shards if fits else plain_shards)(*arrays)


def solution(mesh):
    in_specs = (
        P("req", None),
        P(),
        P(),
        P(),
        P("section", None, None, None),
        P("section", None, "req", None),
        P("section", None, "req"),
        P("section", "req", None, None),
        P("section", "req", None),
        P("section", None, "req", None),
    )
    out_specs = P("req", "section")
    return jax.shard_map(shards, mesh=mesh, in_specs=in_specs, out_specs=out_specs, check_vma=False)
```

```python
import functools

import jax
import jax.numpy as jnp
from jax import lax
from jax.experimental import pallas as pl
from jax.experimental.pallas import tpu as pltpu
from jax.sharding import PartitionSpec as P


def from_behind(block, axis, distance):
    devices = range(lax.axis_size(axis))
    route = [(i - distance, i) for i in devices if i - distance in devices]
    return lax.ppermute(block, axis, route)


def spread_2(value, axis, source):
    kept = jnp.where(lax.axis_index(axis) == source, value, 0).astype(value.dtype)
    return lax.psum(kept, axis)


def layer_norm(values):
    row_mean = jnp.mean(values, axis=-1, keepdims=True)
    centered = values - row_mean
    row_var = jnp.mean(centered * centered, axis=-1, keepdims=True)
    return centered * lax.rsqrt(row_var + 1e-06)


def gelu_tanh(values):
    return (
        0.5
        * values
        * (1.0 + jnp.tanh(0.7978845608028654 * (values + 0.044715 * values * values * values)))
    )


def plain_shards(
    latents,
    patch_route,
    request_len,
    span_order,
    modulation,
    w_qkv,
    w_mlp_in,
    w_out_attn,
    w_out_mlp,
    stale_kv,
):
    section_count = lax.axis_size("section")
    req_count = lax.axis_size("req")
    section_index = lax.axis_index("section")
    req_index = lax.axis_index("req")
    patches = patch_route.shape[0]
    span_count = span_order.shape[0]
    span_rows = patches // span_count
    model_width = latents.shape[1]
    col_width = model_width // req_count
    section_cols = model_width // section_count
    req_total = request_len.shape[0]
    heads_dev = w_qkv.shape[2]
    head_dim = w_qkv.shape[3] // 3
    starts = jnp.cumsum(request_len) - request_len
    patch_ids = jnp.arange(patches, dtype=jnp.int32)
    owner_req = jnp.sum((patch_ids[:, None] >= starts[None, :]).astype(jnp.int32), axis=1) - 1
    seq_req = owner_req[patch_route]
    req_ids = jnp.arange(req_total, dtype=jnp.int32)
    mod_table = modulation[0].reshape(req_total, 3 * model_width)
    qkv_weight = w_qkv[0].reshape(model_width, heads_dev * 3 * head_dim)
    mlp_weight = w_mlp_in[0]
    attn_out_weight = w_out_attn[0].reshape(heads_dev * head_dim, model_width)
    mlp_out_weight = w_out_mlp[0]
    spread = lax.all_to_all(latents, "req", split_axis=1, concat_axis=0, tiled=True)
    sequence = spread[patch_route]
    in_width = sequence.shape[1]

    def work(incoming, kv_cache, span_id):
        first_row = span_id * span_rows
        row_req = lax.dynamic_slice_in_dim(seq_req, first_row, span_rows, 0)
        onehot = (row_req[:, None] == req_ids[None, :]).astype(jnp.float32)
        mod_rows = jnp.dot(onehot, mod_table, precision=lax.Precision.HIGHEST).reshape(
            span_rows, 3, model_width
        )
        current = lax.all_gather(incoming, "req", axis=1, tiled=True)
        normed = (
            layer_norm(current.astype(jnp.float32)) * (1.0 + mod_rows[:, 1]) + mod_rows[:, 0]
        ).astype(jnp.bfloat16)
        qkv_rows = jnp.dot(normed, qkv_weight, preferred_element_type=jnp.float32).reshape(
            span_rows, heads_dev, 3 * head_dim
        )
        query_rows = qkv_rows[:, :, :head_dim].astype(jnp.bfloat16)
        fresh_kv = qkv_rows[:, :, head_dim:].astype(jnp.bfloat16)
        kv_cache = lax.dynamic_update_slice_in_dim(kv_cache, fresh_kv, first_row, 0)
        key_rows = kv_cache[:, :, :head_dim]
        value_rows = kv_cache[:, :, head_dim:]
        scores = jnp.einsum(
            "chd,phd->hcp", query_rows, key_rows, preferred_element_type=jnp.float32
        ) / jnp.sqrt(jnp.float32(head_dim))
        same_req = row_req[:, None] == seq_req[None, :]
        scores = jnp.where(same_req[None], scores, -jnp.inf)
        row_top = jnp.max(scores, axis=-1, keepdims=True)
        weights = jnp.exp(scores - row_top)
        weight_sum = jnp.sum(weights, axis=-1, keepdims=True)
        attention = (weights / weight_sum).astype(jnp.bfloat16)
        attended = jnp.einsum(
            "hcp,phd->chd", attention, value_rows, preferred_element_type=jnp.float32
        ).astype(jnp.bfloat16)
        attended = attended.reshape(span_rows, heads_dev * head_dim)
        mlp_act = gelu_tanh(jnp.dot(normed, mlp_weight, preferred_element_type=jnp.float32)).astype(
            jnp.bfloat16
        )
        partial_value = jnp.dot(attended, attn_out_weight, preferred_element_type=jnp.float32)
        partial_value = partial_value + jnp.dot(
            mlp_act, mlp_out_weight, preferred_element_type=jnp.float32
        )
        branch = lax.psum_scatter(
            partial_value.astype(jnp.bfloat16), "req", scatter_dimension=1, tiled=True
        ).astype(jnp.float32)
        gate_cols = lax.dynamic_slice_in_dim(mod_rows[:, 2], req_index * col_width, col_width, 1)
        updated = (incoming.astype(jnp.float32) + gate_cols * branch).astype(jnp.bfloat16)
        return (updated, kv_cache)

    def advance(moment, carry):
        incoming, kv_cache, results = carry
        span_slot = moment - section_index
        active = (span_slot >= 0) & (span_slot < span_count)
        span_id = span_order[jnp.clip(span_slot, 0, span_count - 1)]
        first_row = span_id * span_rows
        entering = lax.dynamic_slice_in_dim(sequence, first_row, span_rows, 0)
        source = jnp.where(section_index == 0, entering, incoming)
        computed, new_cache = work(source, kv_cache, span_id)
        updated = jnp.where(active, computed, jnp.zeros_like(computed))
        kv_cache = jnp.where(active, new_cache, kv_cache)
        store_here = active & (section_index == section_count - 1)
        current = lax.dynamic_slice_in_dim(results, first_row, span_rows, 0)
        results = lax.dynamic_update_slice_in_dim(
            results, jnp.where(store_here, updated, current), first_row, 0
        )
        incoming = from_behind(updated, "section", 1)
        return (incoming, kv_cache, results)

    start_state = (
        jnp.zeros((span_rows, in_width), jnp.bfloat16),
        stale_kv[0],
        jnp.zeros((patches, in_width), jnp.bfloat16),
    )
    last_in, last_cache, results = lax.fori_loop(
        0, span_count + section_count - 1, advance, start_state
    )
    finished = spread_2(results, "section", section_count - 1)
    inverse = jnp.zeros((patches,), jnp.int32).at[patch_route].set(patch_ids)
    unrouted = finished[inverse]
    owned = lax.all_to_all(unrouted, "req", split_axis=0, concat_axis=1, tiled=True)
    return lax.dynamic_slice_in_dim(owned, section_index * section_cols, section_cols, 1)


MESH = pl.DeviceIdType.MESH
F32 = jnp.float32
BF16 = jnp.bfloat16


def dot(left, right, dims=((1,), (0,)), precision=None):
    return lax.dot_general(
        left, right, (dims, ((), ())), precision=precision, preferred_element_type=F32
    )


def relay_kernel(
    sections,
    reqs,
    route_ref,
    len_ref,
    order_ref,
    latents_ref,
    mod_ref,
    stale_ref,
    w_qkv_ref,
    w_in_ref,
    w_attn_ref,
    w_mlp_ref,
    out_ref,
    raw,
    wq,
    wi,
    wo,
    lat,
    xin,
    normed,
    act,
    kv,
    same,
    perm,
    mods,
    part_send,
    part_recv,
    xnew,
    xfin,
    fin_send,
    fin_recv,
    w_sem,
    lat_ssem,
    lat_rsem,
    x_ssem,
    x_rsem,
    p_ssem,
    p_rsem,
    f_ssem,
    f_rsem,
):
    s = lax.axis_index("section")
    r = lax.axis_index("req")
    devices = sections * reqs
    per = sections // reqs
    patches, width = lat.shape
    rows = patches // 2
    cols = width // reqs
    own_rows = patches // reqs
    heads, head_width = w_qkv_ref.shape[1:]
    chunk = 256
    chunk_count = width // chunk
    hd = head_width // 3
    pieces = [(0, cols)] if cols < 512 else [(0, cols - 256), (cols - 256, 256)]
    attn_width = heads * hd
    mlp_width = wi.shape[1]
    req_total = mod_ref.shape[1]

    def raw_load(c):
        at = pl.ds(pl.multiple_of(c * chunk, chunk), chunk)
        return pltpu.make_async_copy(w_qkv_ref.at[at], raw.at[at], w_sem.at[3 + c])

    for c in range(chunk_count):
        raw_load(c).start()
    loads = [pltpu.make_async_copy(w_in_ref, wi, w_sem.at[0])]
    late_loads = [
        pltpu.make_async_copy(w_attn_ref, wo.at[pl.ds(0, attn_width)], w_sem.at[1]),
        pltpu.make_async_copy(w_mlp_ref, wo.at[pl.ds(attn_width, mlp_width)], w_sem.at[2]),
    ]
    for load in loads + late_loads:
        load.start()

    barrier = pltpu.get_barrier_semaphore()
    me = s * reqs + r

    def greet(step, carry):
        target = lax.rem(me + step, devices)
        pl.semaphore_signal(
            barrier,
            inc=1,
            device_id=(lax.div(target, reqs), lax.rem(target, reqs)),
            device_id_type=MESH,
        )
        return carry

    lax.fori_loop(1, devices, greet, 0)
    pl.semaphore_wait(barrier, devices - 1)

    def peer(step):
        if reqs % 2:
            return lax.rem(r + step, reqs)
        across = lax.rem(lax.div(r, 2) + step // 2, reqs // 2)
        return across * 2 + lax.rem(r + step, 2)

    def lat_copy(step):
        mine = lat.at[pl.ds(pl.multiple_of(r * own_rows, own_rows), own_rows)]
        return pltpu.make_async_remote_copy(
            src_ref=latents_ref,
            dst_ref=mine,
            send_sem=lat_ssem.at[step],
            recv_sem=lat_rsem.at[step],
            device_id=(s, peer(step)),
            device_id_type=MESH,
        )

    @pl.when(s == 0)
    def _():
        for step in range(1, reqs):
            lat_copy(step).start()
        lat[pl.ds(pl.multiple_of(r * own_rows, own_rows), own_rows), :] = latents_ref[...]

    place = lax.broadcasted_iota(jnp.int32, (patches, patches), 0)
    lane = lax.broadcasted_iota(jnp.int32, (patches, patches), 1)
    first, second = order_ref[0], order_ref[1]
    position = jnp.where(place < rows, first * rows + place, second * rows + place - rows)
    chosen = lane == position
    route = jnp.sum(
        jnp.where(chosen, jnp.broadcast_to(route_ref[...], chosen.shape), 0).astype(F32),
        axis=1,
        keepdims=True,
    )
    perm[...] = (lane.astype(F32) == route).astype(BF16)
    req_lane = lax.broadcasted_iota(jnp.int32, (patches, req_total), 1)
    owner = jnp.zeros((patches, req_total), F32)
    start = jnp.int32(0)
    for q in range(req_total):
        end = start + len_ref[q]
        inside = (route >= start.astype(F32)) & (route < end.astype(F32))
        owner = jnp.where((req_lane == q) & inside, 1.0, owner)
        start = end
    same[...] = dot(owner, owner, ((1,), (1,)))
    chosen_bf = chosen.astype(F32).astype(BF16)
    stale = stale_ref[...].reshape(patches, heads * 2 * hd)
    stale = dot(chosen_bf[rows:, :], stale).astype(BF16)
    for h in range(heads):
        kv[h, rows:, :] = stale[:, h * 2 * hd : (h + 1) * 2 * hd]
    for k in range(3):
        for c in range(reqs):
            at = pl.ds(c * cols, cols)
            value = dot(owner, mod_ref[k, :, at], precision=lax.Precision.HIGHEST)
            mods[k, :, at] = value + 1.0 if k == 1 else value

    def flatten(c, carry):
        raw_load(c).wait()
        at = pl.ds(pl.multiple_of(c * chunk, chunk), chunk)
        wq[at, :] = raw[at].reshape(chunk, heads * head_width)
        return carry

    lax.fori_loop(0, chunk_count, flatten, 0)

    @pl.when(s == 0)
    def _():
        for step in range(1, reqs):
            lat_copy(step).wait_recv()
        for c in range(reqs):
            entry = dot(perm[...], lat[:, c * cols : (c + 1) * cols]).astype(BF16)
            xin[0, c] = entry[:rows]
            xin[1, c] = entry[rows:]

    def x_copy(p, t, q, source):
        at = pl.ds(*pieces[p])
        return pltpu.make_async_remote_copy(
            src_ref=xnew.at[t, :, at],
            dst_ref=xin.at[t, source, :, at],
            send_sem=x_ssem.at[p, t, q],
            recv_sem=x_rsem.at[p, t, source],
            device_id=(lax.rem(s + 1, sections), q),
            device_id_type=MESH,
        )

    def part_copy(p, t, step):
        at = pl.ds(*pieces[p])
        return pltpu.make_async_remote_copy(
            src_ref=part_send.at[t, step, :, at],
            dst_ref=part_recv.at[t, step, :, at],
            send_sem=p_ssem.at[p, t, step],
            recv_sem=p_rsem.at[p, t, step],
            device_id=(s, peer(step)),
            device_id_type=MESH,
        )

    def slot(t, carry):
        at_rows = pl.ds(pl.multiple_of(t * rows, rows), rows)

        stats = []
        for p, (begin, size) in enumerate(pieces):
            for q in range(reqs):

                @pl.when(s > 0)
                def _():
                    x_copy(p, t, q, q).wait_recv()

            for q in range(reqs):
                value = xin[t, q, :, begin : begin + size].astype(F32)
                mean = jnp.sum(value, axis=1, keepdims=True) / size
                value = value - mean
                stats.append((size, mean, jnp.sum(value * value, axis=1, keepdims=True)))
        mean = sum(size * part for size, part, _ in stats) / width
        square = sum(part + size * (at - mean) * (at - mean) for size, at, part in stats)
        scale = lax.rsqrt(square / width + 1e-06)
        for c in range(reqs):
            at = pl.ds(c * cols, cols)
            value = (xin[t, c].astype(F32) - mean) * scale
            normed[:, at] = (value * mods[1, at_rows, at] + mods[0, at_rows, at]).astype(BF16)

        @pl.when(t == 0)
        def _():
            for load in loads:
                load.wait()

        allowed = same[at_rows, :] > 0.5
        group = 2 if heads % 2 == 0 else 1
        queries = []
        for g in range(heads // group):
            span = group * head_width
            qkv = dot(normed[...], wq[:, g * span : (g + 1) * span])
            for h in range(group):
                begin = h * head_width
                queries.append(qkv[:, begin : begin + hd].astype(BF16))
                fresh = qkv[:, begin + hd : begin + head_width].astype(BF16)
                kv[g * group + h, at_rows, :] = fresh

        piece = mlp_width // 3 if mlp_width % 384 == 0 else mlp_width
        chunks = mlp_width // piece

        def up(c):
            return dot(normed[...], wi[:, c * piece : (c + 1) * piece])

        def keep(c, hidden):
            at = attn_width + c * piece
            act[:, at : at + piece] = gelu_tanh(hidden).astype(BF16)

        scores = [dot(queries[h], kv[h, :, :hd], ((1,), (1,))) for h in range(heads)]
        hidden = up(0)
        attention = []
        for h in range(heads):
            score = jnp.where(allowed, scores[h] * (hd**-0.5), -jnp.inf)
            top = jnp.max(score, axis=1, keepdims=True)
            weights = jnp.exp(score - top)
            weights = weights / jnp.sum(weights, axis=1, keepdims=True)
            attention.append(weights.astype(BF16))
        keep(0, hidden)
        for c in range(1, chunks):
            hidden = up(c)
            if c == 1:
                for h in range(heads):
                    act[:, h * hd : (h + 1) * hd] = dot(attention[h], kv[h, :, hd:]).astype(BF16)
            keep(c, hidden)
        if chunks == 1:
            for h in range(heads):
                act[:, h * hd : (h + 1) * hd] = dot(attention[h], kv[h, :, hd:]).astype(BF16)

        @pl.when(t == 0)
        def _():
            for load in late_loads:
                load.wait()

        for p, (begin, size) in enumerate(pieces):
            for step in [*range(reqs - 1, 0, -1), 0]:
                at = pl.ds(pl.multiple_of(peer(step) * cols + begin, 128), size)
                product = dot(act[...], wo[:, at]).astype(BF16)
                part_send[t, step, :, begin : begin + size] = product
                if step > 0:
                    part_copy(p, t, step).start()
        for p, (begin, size) in enumerate(pieces):
            branch = part_send[t, 0, :, begin : begin + size].astype(F32)
            for step in range(1, reqs):
                part_copy(p, t, step).wait_recv()
                branch = branch + part_recv[t, step, :, begin : begin + size].astype(F32)
            own = pl.ds(pl.multiple_of(r * cols + begin, 128), size)
            gated = mods[2, at_rows, own] * branch
            updated = xin[t, r, :, begin : begin + size].astype(F32) + gated
            xnew[t, :, begin : begin + size] = updated.astype(BF16)

            @pl.when(s < sections - 1)
            def _():
                for step in range(reqs - 1, -1, -1):
                    x_copy(p, t, peer(step), r).start()

        @pl.when(s == sections - 1)
        def _():
            xfin[at_rows, :] = xnew[t]

        return carry

    lax.fori_loop(0, 2, slot, 0)

    last_own = (sections - 1) // per
    is_self = (s == sections - 1) & (r == last_own)

    def fin_copy(u, q):
        return pltpu.make_async_remote_copy(
            src_ref=fin_send.at[u, q],
            dst_ref=fin_recv,
            send_sem=f_ssem.at[u, q],
            recv_sem=f_rsem.at[0],
            device_id=(r * per + u, q),
            device_id_type=MESH,
        )

    def to_self(u, q):
        return (r * per + u == sections - 1) & (r == q)

    @pl.when(s == sections - 1)
    def _():
        done = dot(perm[...], xfin[...], ((0,), (0,))).astype(BF16)
        out_cols = cols // per
        for u in range(per):
            for q in range(reqs):
                block = done[q * own_rows : (q + 1) * own_rows, u * out_cols : (u + 1) * out_cols]
                fin_send[u, q] = block

                @pl.when(to_self(u, q))
                def _():
                    out_ref[...] = block

                @pl.when(jnp.logical_not(to_self(u, q)))
                def _():
                    fin_copy(u, q).start()

    @pl.when(jnp.logical_not(is_self))
    def _():
        fin_copy(0, 0).wait_recv()
        out_ref[...] = fin_recv[...]

    @pl.when(s == sections - 1)
    def _():
        for u in range(per):
            for q in range(reqs):

                @pl.when(jnp.logical_not(to_self(u, q)))
                def _():
                    fin_copy(u, q).wait_send()

    @pl.when(s == 0)
    def _():
        for step in range(1, reqs):
            lat_copy(step).wait_send()

    for p in range(len(pieces)):
        for t in range(2):
            for step in range(1, reqs):
                part_copy(p, t, step).wait_send()

    @pl.when(s < sections - 1)
    def _():
        for p in range(len(pieces)):
            for t in range(2):
                for q in range(reqs):
                    x_copy(p, t, q, r).wait_send()


def relay_shards(
    latents,
    patch_route,
    request_len,
    span_order,
    modulation,
    w_qkv,
    w_mlp_in,
    w_out_attn,
    w_out_mlp,
    stale_kv,
):
    sections = lax.axis_size("section")
    reqs = lax.axis_size("req")
    patches = patch_route.shape[0]
    own_rows, width = latents.shape
    heads, head_width = w_qkv.shape[2:]
    hd = head_width // 3
    mlp_width = w_mlp_in.shape[2]
    rows, cols, per = patches // 2, width // reqs, sections // reqs
    out_cols = width // sections
    vmem = pl.BlockSpec(memory_space=pltpu.VMEM)
    smem = pl.BlockSpec(memory_space=pltpu.SMEM)
    hbm = pl.BlockSpec(memory_space=pl.ANY)
    weights = width * (heads * head_width + mlp_width) + (heads * hd + mlp_width) * width
    return pl.pallas_call(
        functools.partial(relay_kernel, sections, reqs),
        out_shape=jax.ShapeDtypeStruct((own_rows, out_cols), BF16),
        in_specs=[vmem, smem, smem, vmem, vmem, vmem, hbm, hbm, hbm, hbm],
        out_specs=vmem,
        scratch_shapes=[
            pltpu.VMEM((width, heads, head_width), BF16),
            pltpu.VMEM((width, heads * head_width), BF16),
            pltpu.VMEM((width, mlp_width), BF16),
            pltpu.VMEM((heads * hd + mlp_width, width), BF16),
            pltpu.VMEM((patches, width), BF16),
            pltpu.VMEM((2, reqs, rows, cols), BF16),
            pltpu.VMEM((rows, width), BF16),
            pltpu.VMEM((rows, heads * hd + mlp_width), BF16),
            pltpu.VMEM((heads, patches, 2 * hd), BF16),
            pltpu.VMEM((patches, patches), F32),
            pltpu.VMEM((patches, patches), BF16),
            pltpu.VMEM((3, patches, width), F32),
            pltpu.VMEM((2, reqs, rows, cols), BF16),
            pltpu.VMEM((2, reqs, rows, cols), BF16),
            pltpu.VMEM((2, rows, cols), BF16),
            pltpu.VMEM((patches, cols), BF16),
            pltpu.VMEM((per, reqs, own_rows, out_cols), BF16),
            pltpu.VMEM((own_rows, out_cols), BF16),
            pltpu.SemaphoreType.DMA((3 + width // 256,)),
            pltpu.SemaphoreType.DMA((reqs,)),
            pltpu.SemaphoreType.DMA((reqs,)),
            pltpu.SemaphoreType.DMA((2, 2, reqs)),
            pltpu.SemaphoreType.DMA((2, 2, reqs)),
            pltpu.SemaphoreType.DMA((2, 2, reqs)),
            pltpu.SemaphoreType.DMA((2, 2, reqs)),
            pltpu.SemaphoreType.DMA((per, reqs)),
            pltpu.SemaphoreType.DMA((1,)),
        ],
        compiler_params=pltpu.CompilerParams(
            collective_id=0, has_side_effects=True, vmem_limit_bytes=58 * 2**20
        ),
        cost_estimate=pl.CostEstimate(
            flops=2 * patches * weights, bytes_accessed=2 * weights, transcendentals=0
        ),
    )(
        patch_route.reshape(1, patches),
        request_len,
        span_order,
        latents,
        jnp.transpose(modulation[0], (1, 0, 2)),
        stale_kv[0],
        w_qkv[0],
        w_mlp_in[0],
        w_out_attn[0].reshape(heads * hd, width),
        w_out_mlp[0],
    )


def shards(*arrays):
    sections, reqs = lax.axis_size("section"), lax.axis_size("req")
    width, patches = arrays[0].shape[1], arrays[1].shape[0]
    fits = (
        arrays[3].shape[0] == 2
        and sections % reqs == 0
        and width % (sections * 128) == 0
        and patches % (reqs * 16) == 0
    )
    return (relay_shards if fits else plain_shards)(*arrays)


def solution(mesh):
    in_specs = (
        P("req", None),
        P(),
        P(),
        P(),
        P("section", None, None, None),
        P("section", None, "req", None),
        P("section", None, "req"),
        P("section", "req", None, None),
        P("section", "req", None),
        P("section", None, "req", None),
    )
    out_specs = P("req", "section")
    return jax.shard_map(shards, mesh=mesh, in_specs=in_specs, out_specs=out_specs, check_vma=False)
```

```python
import functools

import jax
import jax.numpy as jnp
from jax import lax
from jax.experimental import pallas as pl
from jax.experimental.pallas import tpu as pltpu
from jax.sharding import PartitionSpec as P


def from_behind(block, axis, distance):
    devices = range(lax.axis_size(axis))
    route = [(i - distance, i) for i in devices if i - distance in devices]
    return lax.ppermute(block, axis, route)


def spread_2(value, axis, source):
    kept = jnp.where(lax.axis_index(axis) == source, value, 0).astype(value.dtype)
    return lax.psum(kept, axis)


def layer_norm(values):
    row_mean = jnp.mean(values, axis=-1, keepdims=True)
    centered = values - row_mean
    row_var = jnp.mean(centered * centered, axis=-1, keepdims=True)
    return centered * lax.rsqrt(row_var + 1e-06)


def gelu_tanh(values):
    return (
        0.5
        * values
        * (1.0 + jnp.tanh(0.7978845608028654 * (values + 0.044715 * values * values * values)))
    )


def plain_shards(
    latents,
    patch_route,
    request_len,
    span_order,
    modulation,
    w_qkv,
    w_mlp_in,
    w_out_attn,
    w_out_mlp,
    stale_kv,
):
    section_count = lax.axis_size("section")
    req_count = lax.axis_size("req")
    section_index = lax.axis_index("section")
    req_index = lax.axis_index("req")
    patches = patch_route.shape[0]
    span_count = span_order.shape[0]
    span_rows = patches // span_count
    model_width = latents.shape[1]
    col_width = model_width // req_count
    section_cols = model_width // section_count
    req_total = request_len.shape[0]
    heads_dev = w_qkv.shape[2]
    head_dim = w_qkv.shape[3] // 3
    starts = jnp.cumsum(request_len) - request_len
    patch_ids = jnp.arange(patches, dtype=jnp.int32)
    owner_req = jnp.sum((patch_ids[:, None] >= starts[None, :]).astype(jnp.int32), axis=1) - 1
    seq_req = owner_req[patch_route]
    req_ids = jnp.arange(req_total, dtype=jnp.int32)
    mod_table = modulation[0].reshape(req_total, 3 * model_width)
    qkv_weight = w_qkv[0].reshape(model_width, heads_dev * 3 * head_dim)
    mlp_weight = w_mlp_in[0]
    attn_out_weight = w_out_attn[0].reshape(heads_dev * head_dim, model_width)
    mlp_out_weight = w_out_mlp[0]
    spread = lax.all_to_all(latents, "req", split_axis=1, concat_axis=0, tiled=True)
    sequence = spread[patch_route]
    in_width = sequence.shape[1]

    def work(incoming, kv_cache, span_id):
        first_row = span_id * span_rows
        row_req = lax.dynamic_slice_in_dim(seq_req, first_row, span_rows, 0)
        onehot = (row_req[:, None] == req_ids[None, :]).astype(jnp.float32)
        mod_rows = jnp.dot(onehot, mod_table, precision=lax.Precision.HIGHEST).reshape(
            span_rows, 3, model_width
        )
        current = lax.all_gather(incoming, "req", axis=1, tiled=True)
        normed = (
            layer_norm(current.astype(jnp.float32)) * (1.0 + mod_rows[:, 1]) + mod_rows[:, 0]
        ).astype(jnp.bfloat16)
        qkv_rows = jnp.dot(normed, qkv_weight, preferred_element_type=jnp.float32).reshape(
            span_rows, heads_dev, 3 * head_dim
        )
        query_rows = qkv_rows[:, :, :head_dim].astype(jnp.bfloat16)
        fresh_kv = qkv_rows[:, :, head_dim:].astype(jnp.bfloat16)
        kv_cache = lax.dynamic_update_slice_in_dim(kv_cache, fresh_kv, first_row, 0)
        key_rows = kv_cache[:, :, :head_dim]
        value_rows = kv_cache[:, :, head_dim:]
        scores = jnp.einsum(
            "chd,phd->hcp", query_rows, key_rows, preferred_element_type=jnp.float32
        ) / jnp.sqrt(jnp.float32(head_dim))
        same_req = row_req[:, None] == seq_req[None, :]
        scores = jnp.where(same_req[None], scores, -jnp.inf)
        row_top = jnp.max(scores, axis=-1, keepdims=True)
        weights = jnp.exp(scores - row_top)
        weight_sum = jnp.sum(weights, axis=-1, keepdims=True)
        attention = (weights / weight_sum).astype(jnp.bfloat16)
        attended = jnp.einsum(
            "hcp,phd->chd", attention, value_rows, preferred_element_type=jnp.float32
        ).astype(jnp.bfloat16)
        attended = attended.reshape(span_rows, heads_dev * head_dim)
        mlp_act = gelu_tanh(jnp.dot(normed, mlp_weight, preferred_element_type=jnp.float32)).astype(
            jnp.bfloat16
        )
        partial_value = jnp.dot(attended, attn_out_weight, preferred_element_type=jnp.float32)
        partial_value = partial_value + jnp.dot(
            mlp_act, mlp_out_weight, preferred_element_type=jnp.float32
        )
        branch = lax.psum_scatter(
            partial_value.astype(jnp.bfloat16), "req", scatter_dimension=1, tiled=True
        ).astype(jnp.float32)
        gate_cols = lax.dynamic_slice_in_dim(mod_rows[:, 2], req_index * col_width, col_width, 1)
        updated = (incoming.astype(jnp.float32) + gate_cols * branch).astype(jnp.bfloat16)
        return (updated, kv_cache)

    def advance(moment, carry):
        incoming, kv_cache, results = carry
        span_slot = moment - section_index
        active = (span_slot >= 0) & (span_slot < span_count)
        span_id = span_order[jnp.clip(span_slot, 0, span_count - 1)]
        first_row = span_id * span_rows
        entering = lax.dynamic_slice_in_dim(sequence, first_row, span_rows, 0)
        source = jnp.where(section_index == 0, entering, incoming)
        computed, new_cache = work(source, kv_cache, span_id)
        updated = jnp.where(active, computed, jnp.zeros_like(computed))
        kv_cache = jnp.where(active, new_cache, kv_cache)
        store_here = active & (section_index == section_count - 1)
        current = lax.dynamic_slice_in_dim(results, first_row, span_rows, 0)
        results = lax.dynamic_update_slice_in_dim(
            results, jnp.where(store_here, updated, current), first_row, 0
        )
        incoming = from_behind(updated, "section", 1)
        return (incoming, kv_cache, results)

    start_state = (
        jnp.zeros((span_rows, in_width), jnp.bfloat16),
        stale_kv[0],
        jnp.zeros((patches, in_width), jnp.bfloat16),
    )
    last_in, last_cache, results = lax.fori_loop(
        0, span_count + section_count - 1, advance, start_state
    )
    finished = spread_2(results, "section", section_count - 1)
    inverse = jnp.zeros((patches,), jnp.int32).at[patch_route].set(patch_ids)
    unrouted = finished[inverse]
    owned = lax.all_to_all(unrouted, "req", split_axis=0, concat_axis=1, tiled=True)
    return lax.dynamic_slice_in_dim(owned, section_index * section_cols, section_cols, 1)


MESH = pl.DeviceIdType.MESH
F32 = jnp.float32
BF16 = jnp.bfloat16


def dot(left, right, dims=((1,), (0,)), precision=None):
    return lax.dot_general(
        left, right, (dims, ((), ())), precision=precision, preferred_element_type=F32
    )


def relay_kernel(
    sections,
    reqs,
    route_ref,
    len_ref,
    order_ref,
    latents_ref,
    mod_ref,
    stale_ref,
    w_qkv_ref,
    w_in_ref,
    w_attn_ref,
    w_mlp_ref,
    out_ref,
    raw,
    wq,
    wi,
    wo,
    lat,
    xin,
    normed,
    act,
    kv,
    same,
    perm,
    mods,
    part_send,
    part_recv,
    xnew,
    xfin,
    fin_send,
    fin_recv,
    w_sem,
    lat_ssem,
    lat_rsem,
    x_ssem,
    x_rsem,
    p_ssem,
    p_rsem,
    f_ssem,
    f_rsem,
):
    s = lax.axis_index("section")
    r = lax.axis_index("req")
    devices = sections * reqs
    per = sections // reqs
    patches, width = lat.shape
    rows = patches // 2
    cols = width // reqs
    own_rows = patches // reqs
    heads, head_width = w_qkv_ref.shape[1:]
    chunk = 256
    chunk_count = width // chunk
    hd = head_width // 3
    pieces = [(0, cols)] if cols < 512 else [(0, 256), (256, cols - 256)]
    attn_width = heads * hd
    mlp_width = wi.shape[1]
    req_total = mod_ref.shape[1]

    def raw_load(c):
        at = pl.ds(pl.multiple_of(c * chunk, chunk), chunk)
        return pltpu.make_async_copy(w_qkv_ref.at[at], raw.at[at], w_sem.at[3 + c])

    for c in range(chunk_count):
        raw_load(c).start()
    loads = [
        pltpu.make_async_copy(w_in_ref, wi, w_sem.at[0]),
        pltpu.make_async_copy(w_attn_ref, wo.at[pl.ds(0, attn_width)], w_sem.at[1]),
        pltpu.make_async_copy(w_mlp_ref, wo.at[pl.ds(attn_width, mlp_width)], w_sem.at[2]),
    ]
    for load in loads:
        load.start()

    barrier = pltpu.get_barrier_semaphore()
    me = s * reqs + r

    def greet(step, carry):
        target = lax.rem(me + step, devices)
        pl.semaphore_signal(
            barrier,
            inc=1,
            device_id=(lax.div(target, reqs), lax.rem(target, reqs)),
            device_id_type=MESH,
        )
        return carry

    lax.fori_loop(1, devices, greet, 0)

    def peer(step):
        if reqs % 2:
            return lax.rem(r + step, reqs)
        across = lax.rem(lax.div(r, 2) + step // 2, reqs // 2)
        return across * 2 + lax.rem(r + step, 2)

    def lat_copy(step):
        mine = lat.at[pl.ds(pl.multiple_of(r * own_rows, own_rows), own_rows)]
        return pltpu.make_async_remote_copy(
            src_ref=latents_ref,
            dst_ref=mine,
            send_sem=lat_ssem.at[step],
            recv_sem=lat_rsem.at[step],
            device_id=(s, peer(step)),
            device_id_type=MESH,
        )

    place = lax.broadcasted_iota(jnp.int32, (patches, patches), 0)
    lane = lax.broadcasted_iota(jnp.int32, (patches, patches), 1)
    first, second = order_ref[0], order_ref[1]
    position = jnp.where(place < rows, first * rows + place, second * rows + place - rows)
    chosen = lane == position
    route = jnp.sum(
        jnp.where(chosen, jnp.broadcast_to(route_ref[...], chosen.shape), 0).astype(F32),
        axis=1,
        keepdims=True,
    )
    perm[...] = (lane.astype(F32) == route).astype(BF16)
    req_lane = lax.broadcasted_iota(jnp.int32, (patches, req_total), 1)
    owner = jnp.zeros((patches, req_total), F32)
    start = jnp.int32(0)
    for q in range(req_total):
        end = start + len_ref[q]
        inside = (route >= start.astype(F32)) & (route < end.astype(F32))
        owner = jnp.where((req_lane == q) & inside, 1.0, owner)
        start = end
    pl.semaphore_wait(barrier, devices - 1)

    @pl.when(s == 0)
    def _():
        for step in range(1, reqs):
            lat_copy(step).start()
        lat[pl.ds(pl.multiple_of(r * own_rows, own_rows), own_rows), :] = latents_ref[...]

    same[...] = dot(owner, owner, ((1,), (1,)))
    chosen_bf = chosen.astype(F32).astype(BF16)
    stale = stale_ref[...].reshape(patches, heads * 2 * hd)
    stale = dot(chosen_bf[rows:, :], stale).astype(BF16)
    for h in range(heads):
        kv[h, rows:, :] = stale[:, h * 2 * hd : (h + 1) * 2 * hd]
    owner_bf = owner.astype(BF16)
    owners = jnp.concatenate([owner_bf, owner_bf, owner_bf], axis=1)
    for k in range(3):
        for c in range(reqs):
            at = pl.ds(c * cols, cols)
            table = mod_ref[k, :, at]
            high = table.astype(BF16)
            left = table - high.astype(F32)
            middle = left.astype(BF16)
            low = (left - middle.astype(F32)).astype(BF16)
            value = dot(owners, jnp.concatenate([high, middle, low], axis=0))
            mods[k, :, at] = value + 1.0 if k == 1 else value

    def flatten(c, carry):
        raw_load(c).wait()
        at = pl.ds(pl.multiple_of(c * chunk, chunk), chunk)
        wq[at, :] = raw[at].reshape(chunk, heads * head_width)
        return carry

    lax.fori_loop(0, chunk_count, flatten, 0)
    for load in loads:
        load.wait()

    @pl.when(s == 0)
    def _():
        for step in range(1, reqs):
            lat_copy(step).wait_recv()
        for c in range(reqs):
            entry = dot(perm[...], lat[:, c * cols : (c + 1) * cols]).astype(BF16)
            xin[0, c] = entry[:rows]
            xin[1, c] = entry[rows:]

    def x_copy(p, t, q, source):
        at = pl.ds(*pieces[p])
        return pltpu.make_async_remote_copy(
            src_ref=xnew.at[t, :, at],
            dst_ref=xin.at[t, source, :, at],
            send_sem=x_ssem.at[p, t, q],
            recv_sem=x_rsem.at[p, t, source],
            device_id=(lax.rem(s + 1, sections), q),
            device_id_type=MESH,
        )

    def part_copy(p, t, step):
        at = pl.ds(*pieces[p])
        return pltpu.make_async_remote_copy(
            src_ref=part_send.at[t, step, :, at],
            dst_ref=part_recv.at[t, step, :, at],
            send_sem=p_ssem.at[p, t, step],
            recv_sem=p_rsem.at[p, t, step],
            device_id=(s, peer(step)),
            device_id_type=MESH,
        )

    def slot(t, carry):
        at_rows = pl.ds(pl.multiple_of(t * rows, rows), rows)

        stats = []
        for p, (begin, size) in enumerate(pieces):
            for step in range(reqs):
                q = peer(step)

                @pl.when(s > 0)
                def _():
                    x_copy(p, t, q, q).wait_recv()

                value = xin[t, q, :, begin : begin + size].astype(F32)
                mean = jnp.sum(value, axis=1, keepdims=True) / size
                value = value - mean
                stats.append((size, mean, jnp.sum(value * value, axis=1, keepdims=True)))
        mean = sum(size * part for size, part, _ in stats) / width
        square = sum(part + size * (at - mean) * (at - mean) for size, at, part in stats)
        scale = lax.rsqrt(square / width + 1e-06)
        for c in range(reqs):
            at = pl.ds(c * cols, cols)
            value = (xin[t, c].astype(F32) - mean) * scale
            normed[:, at] = (value * mods[1, at_rows, at] + mods[0, at_rows, at]).astype(BF16)

        allowed = same[at_rows, :] > 0.5
        group = 2 if heads % 2 == 0 else 1
        queries = []
        for g in range(heads // group):
            span = group * head_width
            qkv = dot(normed[...], wq[:, g * span : (g + 1) * span])
            for h in range(group):
                begin = h * head_width
                queries.append(qkv[:, begin : begin + hd].astype(BF16))
                fresh = qkv[:, begin + hd : begin + head_width].astype(BF16)
                kv[g * group + h, at_rows, :] = fresh

        piece = mlp_width // 3 if mlp_width % 384 == 0 else mlp_width
        chunks = mlp_width // piece

        def up(c):
            return dot(normed[...], wi[:, c * piece : (c + 1) * piece])

        def keep(c, hidden):
            at = attn_width + c * piece
            act[:, at : at + piece] = gelu_tanh(hidden).astype(BF16)

        scores = [dot(queries[h], kv[h, :, :hd], ((1,), (1,))) for h in range(heads)]
        hidden = up(0)
        attention = []
        for h in range(heads):
            score = jnp.where(allowed, scores[h] * (hd**-0.5), -jnp.inf)
            top = jnp.max(score, axis=1, keepdims=True)
            weights = jnp.exp(score - top)
            weights = weights / jnp.sum(weights, axis=1, keepdims=True)
            attention.append(weights.astype(BF16))
        keep(0, hidden)
        for c in range(1, chunks):
            hidden = up(c)
            if c == 1:
                for h in range(heads):
                    act[:, h * hd : (h + 1) * hd] = dot(attention[h], kv[h, :, hd:]).astype(BF16)
            keep(c, hidden)
        if chunks == 1:
            for h in range(heads):
                act[:, h * hd : (h + 1) * hd] = dot(attention[h], kv[h, :, hd:]).astype(BF16)

        for p, (begin, size) in enumerate(pieces):
            together = 2 if size <= 256 and reqs % 2 == 0 else 1
            for base in range(reqs - 1, -1, -together):
                steps = range(base, base - together, -1)
                ats = [pl.ds(pl.multiple_of(peer(m) * cols + begin, 128), size) for m in steps]
                taken = [wo[:, at] for at in ats]
                taken = jnp.concatenate(taken, axis=1) if together > 1 else taken[0]
                product = dot(act[...], taken).astype(BF16)
                for m, step in enumerate(steps):
                    part_send[t, step, :, begin : begin + size] = product[
                        :, m * size : (m + 1) * size
                    ]
                    if step > 0:
                        part_copy(p, t, step).start()
        for p, (begin, size) in enumerate(pieces):
            branch = part_send[t, 0, :, begin : begin + size].astype(F32)
            for step in range(1, reqs):
                part_copy(p, t, step).wait_recv()
                branch = branch + part_recv[t, step, :, begin : begin + size].astype(F32)
            own = pl.ds(pl.multiple_of(r * cols + begin, 128), size)
            gated = mods[2, at_rows, own] * branch
            updated = xin[t, r, :, begin : begin + size].astype(F32) + gated
            xnew[t, :, begin : begin + size] = updated.astype(BF16)

            @pl.when(s < sections - 1)
            def _():
                for step in range(reqs - 1, -1, -1):
                    x_copy(p, t, peer(step), r).start()

        @pl.when(s == sections - 1)
        def _():
            xfin[at_rows, :] = xnew[t]

        return carry

    lax.fori_loop(0, 2, slot, 0)

    last_own = (sections - 1) // per
    is_self = (s == sections - 1) & (r == last_own)

    def fin_copy(u, q):
        return pltpu.make_async_remote_copy(
            src_ref=fin_send.at[u, q],
            dst_ref=fin_recv,
            send_sem=f_ssem.at[u, q],
            recv_sem=f_rsem.at[0],
            device_id=(r * per + u, q),
            device_id_type=MESH,
        )

    def to_self(u, q):
        return (r * per + u == sections - 1) & (r == q)

    @pl.when(s == sections - 1)
    def _():
        done = dot(perm[...], xfin[...], ((0,), (0,))).astype(BF16)
        out_cols = cols // per
        for u in range(per):
            for q in range(reqs):
                block = done[q * own_rows : (q + 1) * own_rows, u * out_cols : (u + 1) * out_cols]
                fin_send[u, q] = block

                @pl.when(to_self(u, q))
                def _():
                    out_ref[...] = block

                @pl.when(jnp.logical_not(to_self(u, q)))
                def _():
                    fin_copy(u, q).start()

    @pl.when(jnp.logical_not(is_self))
    def _():
        fin_copy(0, 0).wait_recv()
        out_ref[...] = fin_recv[...]

    @pl.when(s == sections - 1)
    def _():
        for u in range(per):
            for q in range(reqs):

                @pl.when(jnp.logical_not(to_self(u, q)))
                def _():
                    fin_copy(u, q).wait_send()

    @pl.when(s == 0)
    def _():
        for step in range(1, reqs):
            lat_copy(step).wait_send()

    for p in range(len(pieces)):
        for t in range(2):
            for step in range(1, reqs):
                part_copy(p, t, step).wait_send()

    @pl.when(s < sections - 1)
    def _():
        for p in range(len(pieces)):
            for t in range(2):
                for q in range(reqs):
                    x_copy(p, t, q, r).wait_send()


def relay_shards(
    latents,
    patch_route,
    request_len,
    span_order,
    modulation,
    w_qkv,
    w_mlp_in,
    w_out_attn,
    w_out_mlp,
    stale_kv,
):
    sections = lax.axis_size("section")
    reqs = lax.axis_size("req")
    patches = patch_route.shape[0]
    own_rows, width = latents.shape
    heads, head_width = w_qkv.shape[2:]
    hd = head_width // 3
    mlp_width = w_mlp_in.shape[2]
    rows, cols, per = patches // 2, width // reqs, sections // reqs
    out_cols = width // sections
    vmem = pl.BlockSpec(memory_space=pltpu.VMEM)
    smem = pl.BlockSpec(memory_space=pltpu.SMEM)
    hbm = pl.BlockSpec(memory_space=pl.ANY)
    weights = width * (heads * head_width + mlp_width) + (heads * hd + mlp_width) * width
    return pl.pallas_call(
        functools.partial(relay_kernel, sections, reqs),
        out_shape=jax.ShapeDtypeStruct((own_rows, out_cols), BF16),
        in_specs=[vmem, smem, smem, vmem, vmem, vmem, hbm, hbm, hbm, hbm],
        out_specs=vmem,
        scratch_shapes=[
            pltpu.VMEM((width, heads, head_width), BF16),
            pltpu.VMEM((width, heads * head_width), BF16),
            pltpu.VMEM((width, mlp_width), BF16),
            pltpu.VMEM((heads * hd + mlp_width, width), BF16),
            pltpu.VMEM((patches, width), BF16),
            pltpu.VMEM((2, reqs, rows, cols), BF16),
            pltpu.VMEM((rows, width), BF16),
            pltpu.VMEM((rows, heads * hd + mlp_width), BF16),
            pltpu.VMEM((heads, patches, 2 * hd), BF16),
            pltpu.VMEM((patches, patches), F32),
            pltpu.VMEM((patches, patches), BF16),
            pltpu.VMEM((3, patches, width), F32),
            pltpu.VMEM((2, reqs, rows, cols), BF16),
            pltpu.VMEM((2, reqs, rows, cols), BF16),
            pltpu.VMEM((2, rows, cols), BF16),
            pltpu.VMEM((patches, cols), BF16),
            pltpu.VMEM((per, reqs, own_rows, out_cols), BF16),
            pltpu.VMEM((own_rows, out_cols), BF16),
            pltpu.SemaphoreType.DMA((3 + width // 256,)),
            pltpu.SemaphoreType.DMA((reqs,)),
            pltpu.SemaphoreType.DMA((reqs,)),
            pltpu.SemaphoreType.DMA((2, 2, reqs)),
            pltpu.SemaphoreType.DMA((2, 2, reqs)),
            pltpu.SemaphoreType.DMA((2, 2, reqs)),
            pltpu.SemaphoreType.DMA((2, 2, reqs)),
            pltpu.SemaphoreType.DMA((per, reqs)),
            pltpu.SemaphoreType.DMA((1,)),
        ],
        compiler_params=pltpu.CompilerParams(
            collective_id=0, has_side_effects=True, vmem_limit_bytes=58 * 2**20
        ),
        cost_estimate=pl.CostEstimate(
            flops=2 * patches * weights, bytes_accessed=2 * weights, transcendentals=0
        ),
    )(
        patch_route.reshape(1, patches),
        request_len,
        span_order,
        latents,
        jnp.transpose(modulation[0], (1, 0, 2)),
        stale_kv[0],
        w_qkv[0],
        w_mlp_in[0],
        w_out_attn[0].reshape(heads * hd, width),
        w_out_mlp[0],
    )


def shards(*arrays):
    sections, reqs = lax.axis_size("section"), lax.axis_size("req")
    width, patches = arrays[0].shape[1], arrays[1].shape[0]
    fits = (
        arrays[3].shape[0] == 2
        and sections % reqs == 0
        and width % (sections * 128) == 0
        and patches % (reqs * 16) == 0
    )
    return (relay_shards if fits else plain_shards)(*arrays)


def solution(mesh):
    in_specs = (
        P("req", None),
        P(),
        P(),
        P(),
        P("section", None, None, None),
        P("section", None, "req", None),
        P("section", None, "req"),
        P("section", "req", None, None),
        P("section", "req", None),
        P("section", None, "req", None),
    )
    out_specs = P("req", "section")
    return jax.shard_map(shards, mesh=mesh, in_specs=in_specs, out_specs=out_specs, check_vma=False)
```

```python
import functools

import jax
import jax.numpy as jnp
from jax import lax
from jax.experimental import pallas as pl
from jax.experimental.pallas import tpu as pltpu
from jax.sharding import PartitionSpec as P


def from_behind(block, axis, distance):
    devices = range(lax.axis_size(axis))
    route = [(i - distance, i) for i in devices if i - distance in devices]
    return lax.ppermute(block, axis, route)


def spread_2(value, axis, source):
    kept = jnp.where(lax.axis_index(axis) == source, value, 0).astype(value.dtype)
    return lax.psum(kept, axis)


def layer_norm(values):
    row_mean = jnp.mean(values, axis=-1, keepdims=True)
    centered = values - row_mean
    row_var = jnp.mean(centered * centered, axis=-1, keepdims=True)
    return centered * lax.rsqrt(row_var + 1e-06)


def gelu_tanh(values):
    return (
        0.5
        * values
        * (1.0 + jnp.tanh(0.7978845608028654 * (values + 0.044715 * values * values * values)))
    )


def plain_shards(
    latents,
    patch_route,
    request_len,
    span_order,
    modulation,
    w_qkv,
    w_mlp_in,
    w_out_attn,
    w_out_mlp,
    stale_kv,
):
    section_count = lax.axis_size("section")
    req_count = lax.axis_size("req")
    section_index = lax.axis_index("section")
    req_index = lax.axis_index("req")
    patches = patch_route.shape[0]
    span_count = span_order.shape[0]
    span_rows = patches // span_count
    model_width = latents.shape[1]
    col_width = model_width // req_count
    section_cols = model_width // section_count
    req_total = request_len.shape[0]
    heads_dev = w_qkv.shape[2]
    head_dim = w_qkv.shape[3] // 3
    starts = jnp.cumsum(request_len) - request_len
    patch_ids = jnp.arange(patches, dtype=jnp.int32)
    owner_req = jnp.sum((patch_ids[:, None] >= starts[None, :]).astype(jnp.int32), axis=1) - 1
    seq_req = owner_req[patch_route]
    req_ids = jnp.arange(req_total, dtype=jnp.int32)
    mod_table = modulation[0].reshape(req_total, 3 * model_width)
    qkv_weight = w_qkv[0].reshape(model_width, heads_dev * 3 * head_dim)
    mlp_weight = w_mlp_in[0]
    attn_out_weight = w_out_attn[0].reshape(heads_dev * head_dim, model_width)
    mlp_out_weight = w_out_mlp[0]
    spread = lax.all_to_all(latents, "req", split_axis=1, concat_axis=0, tiled=True)
    sequence = spread[patch_route]
    in_width = sequence.shape[1]

    def work(incoming, kv_cache, span_id):
        first_row = span_id * span_rows
        row_req = lax.dynamic_slice_in_dim(seq_req, first_row, span_rows, 0)
        onehot = (row_req[:, None] == req_ids[None, :]).astype(jnp.float32)
        mod_rows = jnp.dot(onehot, mod_table, precision=lax.Precision.HIGHEST).reshape(
            span_rows, 3, model_width
        )
        current = lax.all_gather(incoming, "req", axis=1, tiled=True)
        normed = (
            layer_norm(current.astype(jnp.float32)) * (1.0 + mod_rows[:, 1]) + mod_rows[:, 0]
        ).astype(jnp.bfloat16)
        qkv_rows = jnp.dot(normed, qkv_weight, preferred_element_type=jnp.float32).reshape(
            span_rows, heads_dev, 3 * head_dim
        )
        query_rows = qkv_rows[:, :, :head_dim].astype(jnp.bfloat16)
        fresh_kv = qkv_rows[:, :, head_dim:].astype(jnp.bfloat16)
        kv_cache = lax.dynamic_update_slice_in_dim(kv_cache, fresh_kv, first_row, 0)
        key_rows = kv_cache[:, :, :head_dim]
        value_rows = kv_cache[:, :, head_dim:]
        scores = jnp.einsum(
            "chd,phd->hcp", query_rows, key_rows, preferred_element_type=jnp.float32
        ) / jnp.sqrt(jnp.float32(head_dim))
        same_req = row_req[:, None] == seq_req[None, :]
        scores = jnp.where(same_req[None], scores, -jnp.inf)
        row_top = jnp.max(scores, axis=-1, keepdims=True)
        weights = jnp.exp(scores - row_top)
        weight_sum = jnp.sum(weights, axis=-1, keepdims=True)
        attention = (weights / weight_sum).astype(jnp.bfloat16)
        attended = jnp.einsum(
            "hcp,phd->chd", attention, value_rows, preferred_element_type=jnp.float32
        ).astype(jnp.bfloat16)
        attended = attended.reshape(span_rows, heads_dev * head_dim)
        mlp_act = gelu_tanh(jnp.dot(normed, mlp_weight, preferred_element_type=jnp.float32)).astype(
            jnp.bfloat16
        )
        partial_value = jnp.dot(attended, attn_out_weight, preferred_element_type=jnp.float32)
        partial_value = partial_value + jnp.dot(
            mlp_act, mlp_out_weight, preferred_element_type=jnp.float32
        )
        branch = lax.psum_scatter(
            partial_value.astype(jnp.bfloat16), "req", scatter_dimension=1, tiled=True
        ).astype(jnp.float32)
        gate_cols = lax.dynamic_slice_in_dim(mod_rows[:, 2], req_index * col_width, col_width, 1)
        updated = (incoming.astype(jnp.float32) + gate_cols * branch).astype(jnp.bfloat16)
        return (updated, kv_cache)

    def advance(moment, carry):
        incoming, kv_cache, results = carry
        span_slot = moment - section_index
        active = (span_slot >= 0) & (span_slot < span_count)
        span_id = span_order[jnp.clip(span_slot, 0, span_count - 1)]
        first_row = span_id * span_rows
        entering = lax.dynamic_slice_in_dim(sequence, first_row, span_rows, 0)
        source = jnp.where(section_index == 0, entering, incoming)
        computed, new_cache = work(source, kv_cache, span_id)
        updated = jnp.where(active, computed, jnp.zeros_like(computed))
        kv_cache = jnp.where(active, new_cache, kv_cache)
        store_here = active & (section_index == section_count - 1)
        current = lax.dynamic_slice_in_dim(results, first_row, span_rows, 0)
        results = lax.dynamic_update_slice_in_dim(
            results, jnp.where(store_here, updated, current), first_row, 0
        )
        incoming = from_behind(updated, "section", 1)
        return (incoming, kv_cache, results)

    start_state = (
        jnp.zeros((span_rows, in_width), jnp.bfloat16),
        stale_kv[0],
        jnp.zeros((patches, in_width), jnp.bfloat16),
    )
    last_in, last_cache, results = lax.fori_loop(
        0, span_count + section_count - 1, advance, start_state
    )
    finished = spread_2(results, "section", section_count - 1)
    inverse = jnp.zeros((patches,), jnp.int32).at[patch_route].set(patch_ids)
    unrouted = finished[inverse]
    owned = lax.all_to_all(unrouted, "req", split_axis=0, concat_axis=1, tiled=True)
    return lax.dynamic_slice_in_dim(owned, section_index * section_cols, section_cols, 1)


MESH = pl.DeviceIdType.MESH
F32 = jnp.float32
BF16 = jnp.bfloat16


def dot(left, right, dims=((1,), (0,)), precision=None):
    return lax.dot_general(
        left, right, (dims, ((), ())), precision=precision, preferred_element_type=F32
    )


def relay_kernel(
    sections,
    reqs,
    route_ref,
    len_ref,
    order_ref,
    latents_ref,
    mod_ref,
    stale_ref,
    w_qkv_ref,
    w_in_ref,
    w_attn_ref,
    w_mlp_ref,
    out_ref,
    raw,
    wq,
    wi,
    wo,
    lat,
    xin,
    normed,
    act,
    kv,
    same,
    perm,
    mods,
    fixes,
    early,
    part_send,
    part_recv,
    xnew,
    xfin,
    fin_send,
    fin_recv,
    w_sem,
    lat_ssem,
    lat_rsem,
    x_ssem,
    x_rsem,
    p_ssem,
    p_rsem,
    f_ssem,
    f_rsem,
):
    s = lax.axis_index("section")
    r = lax.axis_index("req")
    devices = sections * reqs
    per = sections // reqs
    patches, width = lat.shape
    rows = patches // 2
    cols = width // reqs
    own_rows = patches // reqs
    heads, head_width = w_qkv_ref.shape[1:]
    chunk = 256
    chunk_count = width // chunk
    hd = head_width // 3
    pieces = [(0, cols)] if cols < 512 else [(0, 256), (256, cols - 256)]
    attn_width = heads * hd
    mlp_width = wi.shape[1]
    req_total = mod_ref.shape[1]

    def raw_load(c):
        at = pl.ds(pl.multiple_of(c * chunk, chunk), chunk)
        return pltpu.make_async_copy(w_qkv_ref.at[at], raw.at[at], w_sem.at[3 + c])

    for c in range(chunk_count):
        raw_load(c).start()
    loads = [
        pltpu.make_async_copy(w_in_ref, wi, w_sem.at[0]),
        pltpu.make_async_copy(w_attn_ref, wo.at[pl.ds(0, attn_width)], w_sem.at[1]),
        pltpu.make_async_copy(w_mlp_ref, wo.at[pl.ds(attn_width, mlp_width)], w_sem.at[2]),
    ]
    for load in loads:
        load.start()

    barrier = pltpu.get_barrier_semaphore()
    me = s * reqs + r

    def greet(step, carry):
        target = lax.rem(me + step, devices)
        pl.semaphore_signal(
            barrier,
            inc=1,
            device_id=(lax.div(target, reqs), lax.rem(target, reqs)),
            device_id_type=MESH,
        )
        return carry

    lax.fori_loop(1, devices, greet, 0)

    def peer(step):
        if reqs % 2:
            return lax.rem(r + step, reqs)
        across = lax.rem(lax.div(r, 2) + step // 2, reqs // 2)
        return across * 2 + lax.rem(r + step, 2)

    def lat_copy(step):
        mine = lat.at[pl.ds(pl.multiple_of(r * own_rows, own_rows), own_rows)]
        return pltpu.make_async_remote_copy(
            src_ref=latents_ref,
            dst_ref=mine,
            send_sem=lat_ssem.at[step],
            recv_sem=lat_rsem.at[step],
            device_id=(s, peer(step)),
            device_id_type=MESH,
        )

    place = lax.broadcasted_iota(jnp.int32, (patches, patches), 0)
    lane = lax.broadcasted_iota(jnp.int32, (patches, patches), 1)
    first, second = order_ref[0], order_ref[1]
    position = jnp.where(place < rows, first * rows + place, second * rows + place - rows)
    chosen = lane == position
    route = jnp.sum(
        jnp.where(chosen, jnp.broadcast_to(route_ref[...], chosen.shape), 0).astype(F32),
        axis=1,
        keepdims=True,
    )
    perm[...] = (lane.astype(F32) == route).astype(BF16)
    req_lane = lax.broadcasted_iota(jnp.int32, (patches, req_total), 1)
    owner = jnp.zeros((patches, req_total), F32)
    start = jnp.int32(0)
    for q in range(req_total):
        end = start + len_ref[q]
        inside = (route >= start.astype(F32)) & (route < end.astype(F32))
        owner = jnp.where((req_lane == q) & inside, 1.0, owner)
        start = end
    pl.semaphore_wait(barrier, devices - 1)

    @pl.when(s == 0)
    def _():
        for step in range(1, reqs):
            lat_copy(step).start()
        lat[pl.ds(pl.multiple_of(r * own_rows, own_rows), own_rows), :] = latents_ref[...]

    same[...] = dot(owner, owner, ((1,), (1,)))
    chosen_bf = chosen.astype(F32).astype(BF16)
    stale = stale_ref[...].reshape(patches, heads * 2 * hd)
    stale = dot(chosen_bf[rows:, :], stale).astype(BF16)
    for h in range(heads):
        kv[h, rows:, :] = stale[:, h * 2 * hd : (h + 1) * 2 * hd]
    owner_bf = owner.astype(BF16)
    owners = jnp.concatenate([owner_bf, owner_bf, owner_bf], axis=1)

    def expand(table):
        high = table.astype(BF16)
        left = table - high.astype(F32)
        middle = left.astype(BF16)
        low = (left - middle.astype(F32)).astype(BF16)
        return dot(owners, jnp.concatenate([high, middle, low], axis=0))

    for k in (1, 2):
        for c in range(reqs):
            at = pl.ds(c * cols, cols)
            value = expand(mod_ref[k, :, at])
            mods[k - 1, :, at] = value + 1.0 if k == 1 else value

    def flatten(c, carry):
        raw_load(c).wait()
        at = pl.ds(pl.multiple_of(c * chunk, chunk), chunk)
        wq[at, :] = raw[at].reshape(chunk, heads * head_width)
        return carry

    lax.fori_loop(0, chunk_count, flatten, 0)
    for load in loads:
        load.wait()
    qkv_width = heads * head_width
    group = 2 if heads % 2 == 0 else 1
    span = group * head_width
    piece = mlp_width // 3 if mlp_width % 384 == 0 else mlp_width
    qkv_parts = [(wq, at, span, at) for at in range(0, qkv_width, span)]
    mlp_parts = [(wi, at, piece, qkv_width + at) for at in range(0, mlp_width, piece)]
    lines = jnp.concatenate([mod_ref[1] + 1.0, mod_ref[0]], axis=0).astype(BF16)
    for weight, at, size, to in qkv_parts + mlp_parts:
        lined = dot(lines, weight[:, at : at + size])
        fixes[0, :, to : to + size] = expand(lined[:req_total])
        fixes[1, :, to : to + size] = expand(lined[req_total:])

    @pl.when(s == 0)
    def _():
        for step in range(1, reqs):
            lat_copy(step).wait_recv()
        for c in range(reqs):
            entry = dot(perm[...], lat[:, c * cols : (c + 1) * cols]).astype(BF16)
            xin[0, c] = entry[:rows]
            xin[1, c] = entry[rows:]

    def x_copy(p, t, q, source):
        at = pl.ds(*pieces[p])
        return pltpu.make_async_remote_copy(
            src_ref=xnew.at[t, :, at],
            dst_ref=xin.at[t, source, :, at],
            send_sem=x_ssem.at[p, t, q],
            recv_sem=x_rsem.at[p, t, source],
            device_id=(lax.rem(s + 1, sections), q),
            device_id_type=MESH,
        )

    def part_copy(p, t, step):
        at = pl.ds(*pieces[p])
        return pltpu.make_async_remote_copy(
            src_ref=part_send.at[t, step, :, at],
            dst_ref=part_recv.at[t, step, :, at],
            send_sem=p_ssem.at[p, t, step],
            recv_sem=p_rsem.at[p, t, step],
            device_id=(s, peer(step)),
            device_id_type=MESH,
        )

    def slot(t, carry):
        at_rows = pl.ds(pl.multiple_of(t * rows, rows), rows)

        def push(p, part):
            begin, size = pieces[p]
            weight, at, part_size, _ = part
            return sum(
                dot(
                    normed[:, c * cols + begin : c * cols + begin + size],
                    weight[c * cols + begin : c * cols + begin + size, at : at + part_size],
                )
                for c in range(reqs)
            )

        stats = []
        base = None
        for p, (begin, size) in enumerate(pieces):
            for step in range(reqs):
                q = peer(step)

                @pl.when(s > 0)
                def _():
                    x_copy(p, t, q, q).wait_recv()

                value = xin[t, q, :, begin : begin + size].astype(F32)
                mean = jnp.sum(value, axis=1, keepdims=True) / size
                value = value - mean
                stats.append((size, mean, jnp.sum(value * value, axis=1, keepdims=True)))
            if base is None:
                base = sum(part for _, part, _ in stats) / reqs
            for c in range(reqs):
                at = pl.ds(c * cols + begin, size)
                value = xin[t, c, :, begin : begin + size].astype(F32) - base
                normed[:, at] = (value * mods[0, at_rows, at]).astype(BF16)
            if p < len(pieces) - 1:
                for part in qkv_parts + mlp_parts:
                    at = pl.ds(part[3], part[2])
                    pushed = push(p, part)
                    early[:, at] = pushed if p == 0 else early[:, at] + pushed
        mean = sum(size * part for size, part, _ in stats) / width
        square = sum(part + size * (at - mean) * (at - mean) for size, at, part in stats)
        scale = lax.rsqrt(square / width + 1e-06)
        offset = mean - base

        def product(part):
            at = pl.ds(part[3], part[2])
            value = push(len(pieces) - 1, part)
            if len(pieces) > 1:
                value = value + early[:, at]
            return (value - offset * fixes[0, at_rows, at]) * scale + fixes[1, at_rows, at]

        allowed = same[at_rows, :] > 0.5
        queries = []
        for g in range(heads // group):
            qkv = product(qkv_parts[g])
            for h in range(group):
                begin = h * head_width
                queries.append(qkv[:, begin : begin + hd].astype(BF16))
                fresh = qkv[:, begin + hd : begin + head_width].astype(BF16)
                kv[g * group + h, at_rows, :] = fresh

        chunks = len(mlp_parts)

        def up(c):
            return product(mlp_parts[c])

        def keep(c, hidden):
            at = attn_width + c * piece
            act[:, at : at + piece] = gelu_tanh(hidden).astype(BF16)

        scores = [dot(queries[h], kv[h, :, :hd], ((1,), (1,))) for h in range(heads)]
        hidden = up(0)
        attention = []
        for h in range(heads):
            score = jnp.where(allowed, scores[h] * (hd**-0.5), -jnp.inf)
            top = jnp.max(score, axis=1, keepdims=True)
            weights = jnp.exp(score - top)
            weights = weights / jnp.sum(weights, axis=1, keepdims=True)
            attention.append(weights.astype(BF16))
        keep(0, hidden)
        for c in range(1, chunks):
            hidden = up(c)
            if c == 1:
                for h in range(heads):
                    act[:, h * hd : (h + 1) * hd] = dot(attention[h], kv[h, :, hd:]).astype(BF16)
            keep(c, hidden)
        if chunks == 1:
            for h in range(heads):
                act[:, h * hd : (h + 1) * hd] = dot(attention[h], kv[h, :, hd:]).astype(BF16)

        for p, (begin, size) in enumerate(pieces):
            together = 2 if size <= 256 and reqs % 2 == 0 else 1
            for base in range(reqs - 1, -1, -together):
                steps = range(base, base - together, -1)
                ats = [pl.ds(pl.multiple_of(peer(m) * cols + begin, 128), size) for m in steps]
                taken = [wo[:, at] for at in ats]
                taken = jnp.concatenate(taken, axis=1) if together > 1 else taken[0]
                shares = dot(act[...], taken).astype(BF16)
                for m, step in enumerate(steps):
                    part_send[t, step, :, begin : begin + size] = shares[
                        :, m * size : (m + 1) * size
                    ]
                    if step > 0:
                        part_copy(p, t, step).start()
        for p, (begin, size) in enumerate(pieces):
            branch = part_send[t, 0, :, begin : begin + size].astype(F32)
            for step in range(1, reqs):
                part_copy(p, t, step).wait_recv()
                branch = branch + part_recv[t, step, :, begin : begin + size].astype(F32)
            own = pl.ds(pl.multiple_of(r * cols + begin, 128), size)
            gated = mods[1, at_rows, own] * branch
            updated = xin[t, r, :, begin : begin + size].astype(F32) + gated
            xnew[t, :, begin : begin + size] = updated.astype(BF16)

            @pl.when(s < sections - 1)
            def _():
                for step in range(reqs - 1, -1, -1):
                    x_copy(p, t, peer(step), r).start()

        @pl.when(s == sections - 1)
        def _():
            xfin[at_rows, :] = xnew[t]

        return carry

    lax.fori_loop(0, 2, slot, 0)

    last_own = (sections - 1) // per
    is_self = (s == sections - 1) & (r == last_own)

    def fin_copy(u, q):
        return pltpu.make_async_remote_copy(
            src_ref=fin_send.at[u, q],
            dst_ref=fin_recv,
            send_sem=f_ssem.at[u, q],
            recv_sem=f_rsem.at[0],
            device_id=(r * per + u, q),
            device_id_type=MESH,
        )

    def to_self(u, q):
        return (r * per + u == sections - 1) & (r == q)

    @pl.when(s == sections - 1)
    def _():
        done = dot(perm[...], xfin[...], ((0,), (0,))).astype(BF16)
        out_cols = cols // per
        for u in range(per):
            for q in range(reqs):
                block = done[q * own_rows : (q + 1) * own_rows, u * out_cols : (u + 1) * out_cols]
                fin_send[u, q] = block

                @pl.when(to_self(u, q))
                def _():
                    out_ref[...] = block

                @pl.when(jnp.logical_not(to_self(u, q)))
                def _():
                    fin_copy(u, q).start()

    @pl.when(jnp.logical_not(is_self))
    def _():
        fin_copy(0, 0).wait_recv()
        out_ref[...] = fin_recv[...]

    @pl.when(s == sections - 1)
    def _():
        for u in range(per):
            for q in range(reqs):

                @pl.when(jnp.logical_not(to_self(u, q)))
                def _():
                    fin_copy(u, q).wait_send()

    @pl.when(s == 0)
    def _():
        for step in range(1, reqs):
            lat_copy(step).wait_send()

    for p in range(len(pieces)):
        for t in range(2):
            for step in range(1, reqs):
                part_copy(p, t, step).wait_send()

    @pl.when(s < sections - 1)
    def _():
        for p in range(len(pieces)):
            for t in range(2):
                for q in range(reqs):
                    x_copy(p, t, q, r).wait_send()


def relay_shards(
    latents,
    patch_route,
    request_len,
    span_order,
    modulation,
    w_qkv,
    w_mlp_in,
    w_out_attn,
    w_out_mlp,
    stale_kv,
):
    sections = lax.axis_size("section")
    reqs = lax.axis_size("req")
    patches = patch_route.shape[0]
    own_rows, width = latents.shape
    heads, head_width = w_qkv.shape[2:]
    hd = head_width // 3
    mlp_width = w_mlp_in.shape[2]
    rows, cols, per = patches // 2, width // reqs, sections // reqs
    out_cols = width // sections
    vmem = pl.BlockSpec(memory_space=pltpu.VMEM)
    smem = pl.BlockSpec(memory_space=pltpu.SMEM)
    hbm = pl.BlockSpec(memory_space=pl.ANY)
    weights = width * (heads * head_width + mlp_width) + (heads * hd + mlp_width) * width
    return pl.pallas_call(
        functools.partial(relay_kernel, sections, reqs),
        out_shape=jax.ShapeDtypeStruct((own_rows, out_cols), BF16),
        in_specs=[vmem, smem, smem, vmem, vmem, vmem, hbm, hbm, hbm, hbm],
        out_specs=vmem,
        scratch_shapes=[
            pltpu.VMEM((width, heads, head_width), BF16),
            pltpu.VMEM((width, heads * head_width), BF16),
            pltpu.VMEM((width, mlp_width), BF16),
            pltpu.VMEM((heads * hd + mlp_width, width), BF16),
            pltpu.VMEM((patches, width), BF16),
            pltpu.VMEM((2, reqs, rows, cols), BF16),
            pltpu.VMEM((rows, width), BF16),
            pltpu.VMEM((rows, heads * hd + mlp_width), BF16),
            pltpu.VMEM((heads, patches, 2 * hd), BF16),
            pltpu.VMEM((patches, patches), F32),
            pltpu.VMEM((patches, patches), BF16),
            pltpu.VMEM((2, patches, width), F32),
            pltpu.VMEM((2, patches, heads * head_width + mlp_width), F32),
            pltpu.VMEM((rows, heads * head_width + mlp_width), F32),
            pltpu.VMEM((2, reqs, rows, cols), BF16),
            pltpu.VMEM((2, reqs, rows, cols), BF16),
            pltpu.VMEM((2, rows, cols), BF16),
            pltpu.VMEM((patches, cols), BF16),
            pltpu.VMEM((per, reqs, own_rows, out_cols), BF16),
            pltpu.VMEM((own_rows, out_cols), BF16),
            pltpu.SemaphoreType.DMA((3 + width // 256,)),
            pltpu.SemaphoreType.DMA((reqs,)),
            pltpu.SemaphoreType.DMA((reqs,)),
            pltpu.SemaphoreType.DMA((2, 2, reqs)),
            pltpu.SemaphoreType.DMA((2, 2, reqs)),
            pltpu.SemaphoreType.DMA((2, 2, reqs)),
            pltpu.SemaphoreType.DMA((2, 2, reqs)),
            pltpu.SemaphoreType.DMA((per, reqs)),
            pltpu.SemaphoreType.DMA((1,)),
        ],
        compiler_params=pltpu.CompilerParams(
            collective_id=0, has_side_effects=True, vmem_limit_bytes=58 * 2**20
        ),
        cost_estimate=pl.CostEstimate(
            flops=2 * patches * weights, bytes_accessed=2 * weights, transcendentals=0
        ),
    )(
        patch_route.reshape(1, patches),
        request_len,
        span_order,
        latents,
        jnp.transpose(modulation[0], (1, 0, 2)),
        stale_kv[0],
        w_qkv[0],
        w_mlp_in[0],
        w_out_attn[0].reshape(heads * hd, width),
        w_out_mlp[0],
    )


def shards(*arrays):
    sections, reqs = lax.axis_size("section"), lax.axis_size("req")
    width, patches = arrays[0].shape[1], arrays[1].shape[0]
    fits = (
        arrays[3].shape[0] == 2
        and sections % reqs == 0
        and width % (sections * 128) == 0
        and patches % (reqs * 16) == 0
    )
    return (relay_shards if fits else plain_shards)(*arrays)


def solution(mesh):
    in_specs = (
        P("req", None),
        P(),
        P(),
        P(),
        P("section", None, None, None),
        P("section", None, "req", None),
        P("section", None, "req"),
        P("section", "req", None, None),
        P("section", "req", None),
        P("section", None, "req", None),
    )
    out_specs = P("req", "section")
    return jax.shard_map(shards, mesh=mesh, in_specs=in_specs, out_specs=out_specs, check_vma=False)
```

```python
import functools

import jax
import jax.numpy as jnp
from jax import lax
from jax.experimental import pallas as pl
from jax.experimental.pallas import tpu as pltpu
from jax.sharding import PartitionSpec as P


def from_behind(block, axis, distance):
    devices = range(lax.axis_size(axis))
    route = [(i - distance, i) for i in devices if i - distance in devices]
    return lax.ppermute(block, axis, route)


def spread_2(value, axis, source):
    kept = jnp.where(lax.axis_index(axis) == source, value, 0).astype(value.dtype)
    return lax.psum(kept, axis)


def layer_norm(values):
    row_mean = jnp.mean(values, axis=-1, keepdims=True)
    centered = values - row_mean
    row_var = jnp.mean(centered * centered, axis=-1, keepdims=True)
    return centered * lax.rsqrt(row_var + 1e-06)


def gelu_tanh(values):
    return (
        0.5
        * values
        * (1.0 + jnp.tanh(0.7978845608028654 * (values + 0.044715 * values * values * values)))
    )


def plain_shards(
    latents,
    patch_route,
    request_len,
    span_order,
    modulation,
    w_qkv,
    w_mlp_in,
    w_out_attn,
    w_out_mlp,
    stale_kv,
):
    section_count = lax.axis_size("section")
    req_count = lax.axis_size("req")
    section_index = lax.axis_index("section")
    req_index = lax.axis_index("req")
    patches = patch_route.shape[0]
    span_count = span_order.shape[0]
    span_rows = patches // span_count
    model_width = latents.shape[1]
    col_width = model_width // req_count
    section_cols = model_width // section_count
    req_total = request_len.shape[0]
    heads_dev = w_qkv.shape[2]
    head_dim = w_qkv.shape[3] // 3
    starts = jnp.cumsum(request_len) - request_len
    patch_ids = jnp.arange(patches, dtype=jnp.int32)
    owner_req = jnp.sum((patch_ids[:, None] >= starts[None, :]).astype(jnp.int32), axis=1) - 1
    seq_req = owner_req[patch_route]
    req_ids = jnp.arange(req_total, dtype=jnp.int32)
    mod_table = modulation[0].reshape(req_total, 3 * model_width)
    qkv_weight = w_qkv[0].reshape(model_width, heads_dev * 3 * head_dim)
    mlp_weight = w_mlp_in[0]
    attn_out_weight = w_out_attn[0].reshape(heads_dev * head_dim, model_width)
    mlp_out_weight = w_out_mlp[0]
    spread = lax.all_to_all(latents, "req", split_axis=1, concat_axis=0, tiled=True)
    sequence = spread[patch_route]
    in_width = sequence.shape[1]

    def work(incoming, kv_cache, span_id):
        first_row = span_id * span_rows
        row_req = lax.dynamic_slice_in_dim(seq_req, first_row, span_rows, 0)
        onehot = (row_req[:, None] == req_ids[None, :]).astype(jnp.float32)
        mod_rows = jnp.dot(onehot, mod_table, precision=lax.Precision.HIGHEST).reshape(
            span_rows, 3, model_width
        )
        current = lax.all_gather(incoming, "req", axis=1, tiled=True)
        normed = (
            layer_norm(current.astype(jnp.float32)) * (1.0 + mod_rows[:, 1]) + mod_rows[:, 0]
        ).astype(jnp.bfloat16)
        qkv_rows = jnp.dot(normed, qkv_weight, preferred_element_type=jnp.float32).reshape(
            span_rows, heads_dev, 3 * head_dim
        )
        query_rows = qkv_rows[:, :, :head_dim].astype(jnp.bfloat16)
        fresh_kv = qkv_rows[:, :, head_dim:].astype(jnp.bfloat16)
        kv_cache = lax.dynamic_update_slice_in_dim(kv_cache, fresh_kv, first_row, 0)
        key_rows = kv_cache[:, :, :head_dim]
        value_rows = kv_cache[:, :, head_dim:]
        scores = jnp.einsum(
            "chd,phd->hcp", query_rows, key_rows, preferred_element_type=jnp.float32
        ) / jnp.sqrt(jnp.float32(head_dim))
        same_req = row_req[:, None] == seq_req[None, :]
        scores = jnp.where(same_req[None], scores, -jnp.inf)
        row_top = jnp.max(scores, axis=-1, keepdims=True)
        weights = jnp.exp(scores - row_top)
        weight_sum = jnp.sum(weights, axis=-1, keepdims=True)
        attention = (weights / weight_sum).astype(jnp.bfloat16)
        attended = jnp.einsum(
            "hcp,phd->chd", attention, value_rows, preferred_element_type=jnp.float32
        ).astype(jnp.bfloat16)
        attended = attended.reshape(span_rows, heads_dev * head_dim)
        mlp_act = gelu_tanh(jnp.dot(normed, mlp_weight, preferred_element_type=jnp.float32)).astype(
            jnp.bfloat16
        )
        partial_value = jnp.dot(attended, attn_out_weight, preferred_element_type=jnp.float32)
        partial_value = partial_value + jnp.dot(
            mlp_act, mlp_out_weight, preferred_element_type=jnp.float32
        )
        branch = lax.psum_scatter(
            partial_value.astype(jnp.bfloat16), "req", scatter_dimension=1, tiled=True
        ).astype(jnp.float32)
        gate_cols = lax.dynamic_slice_in_dim(mod_rows[:, 2], req_index * col_width, col_width, 1)
        updated = (incoming.astype(jnp.float32) + gate_cols * branch).astype(jnp.bfloat16)
        return (updated, kv_cache)

    def advance(moment, carry):
        incoming, kv_cache, results = carry
        span_slot = moment - section_index
        active = (span_slot >= 0) & (span_slot < span_count)
        span_id = span_order[jnp.clip(span_slot, 0, span_count - 1)]
        first_row = span_id * span_rows
        entering = lax.dynamic_slice_in_dim(sequence, first_row, span_rows, 0)
        source = jnp.where(section_index == 0, entering, incoming)
        computed, new_cache = work(source, kv_cache, span_id)
        updated = jnp.where(active, computed, jnp.zeros_like(computed))
        kv_cache = jnp.where(active, new_cache, kv_cache)
        store_here = active & (section_index == section_count - 1)
        current = lax.dynamic_slice_in_dim(results, first_row, span_rows, 0)
        results = lax.dynamic_update_slice_in_dim(
            results, jnp.where(store_here, updated, current), first_row, 0
        )
        incoming = from_behind(updated, "section", 1)
        return (incoming, kv_cache, results)

    start_state = (
        jnp.zeros((span_rows, in_width), jnp.bfloat16),
        stale_kv[0],
        jnp.zeros((patches, in_width), jnp.bfloat16),
    )
    last_in, last_cache, results = lax.fori_loop(
        0, span_count + section_count - 1, advance, start_state
    )
    finished = spread_2(results, "section", section_count - 1)
    inverse = jnp.zeros((patches,), jnp.int32).at[patch_route].set(patch_ids)
    unrouted = finished[inverse]
    owned = lax.all_to_all(unrouted, "req", split_axis=0, concat_axis=1, tiled=True)
    return lax.dynamic_slice_in_dim(owned, section_index * section_cols, section_cols, 1)


MESH = pl.DeviceIdType.MESH
F32 = jnp.float32
BF16 = jnp.bfloat16


def dot(left, right, dims=((1,), (0,)), precision=None):
    return lax.dot_general(
        left, right, (dims, ((), ())), precision=precision, preferred_element_type=F32
    )


def pieces_of(cols):
    size = 256 if cols % 256 == 0 else cols
    return [(begin, size) for begin in range(0, cols, size)]


def relay_kernel(
    sections,
    reqs,
    route_ref,
    len_ref,
    order_ref,
    latents_ref,
    mod_ref,
    stale_ref,
    w_qkv_ref,
    w_in_ref,
    w_attn_ref,
    w_mlp_ref,
    out_ref,
    raw,
    wq,
    wi,
    wo,
    lat,
    xin,
    normed,
    act,
    kv,
    same,
    perm,
    mods,
    fixes,
    early,
    part_send,
    part_recv,
    xnew,
    xfin,
    fin_send,
    fin_recv,
    w_sem,
    lat_ssem,
    lat_rsem,
    x_ssem,
    x_rsem,
    p_ssem,
    p_rsem,
    f_ssem,
    f_rsem,
):
    s = lax.axis_index("section")
    r = lax.axis_index("req")
    devices = sections * reqs
    per = sections // reqs
    patches, width = lat.shape
    rows = patches // 2
    cols = width // reqs
    own_rows = patches // reqs
    heads, head_width = w_qkv_ref.shape[1:]
    chunk = 256
    chunk_count = width // chunk
    hd = head_width // 3
    pieces = pieces_of(cols)
    attn_width = heads * hd
    mlp_width = wi.shape[1]
    req_total = mod_ref.shape[1]

    def raw_load(c):
        at = pl.ds(pl.multiple_of(c * chunk, chunk), chunk)
        return pltpu.make_async_copy(w_qkv_ref.at[at], raw.at[at], w_sem.at[3 + c])

    for c in range(chunk_count):
        raw_load(c).start()
    loads = [
        pltpu.make_async_copy(w_in_ref, wi, w_sem.at[0]),
        pltpu.make_async_copy(w_attn_ref, wo.at[pl.ds(0, attn_width)], w_sem.at[1]),
        pltpu.make_async_copy(w_mlp_ref, wo.at[pl.ds(attn_width, mlp_width)], w_sem.at[2]),
    ]
    for load in loads:
        load.start()

    barrier = pltpu.get_barrier_semaphore()
    me = s * reqs + r

    def greet(step, carry):
        target = lax.rem(me + step, devices)
        pl.semaphore_signal(
            barrier,
            inc=1,
            device_id=(lax.div(target, reqs), lax.rem(target, reqs)),
            device_id_type=MESH,
        )
        return carry

    lax.fori_loop(1, devices, greet, 0)

    def peer(step):
        if reqs % 2:
            return lax.rem(r + step, reqs)
        across = lax.rem(lax.div(r, 2) + step // 2, reqs // 2)
        return across * 2 + lax.rem(r + step, 2)

    def lat_copy(step):
        mine = lat.at[pl.ds(pl.multiple_of(r * own_rows, own_rows), own_rows)]
        return pltpu.make_async_remote_copy(
            src_ref=latents_ref,
            dst_ref=mine,
            send_sem=lat_ssem.at[step],
            recv_sem=lat_rsem.at[step],
            device_id=(s, peer(step)),
            device_id_type=MESH,
        )

    place = lax.broadcasted_iota(jnp.int32, (patches, patches), 0)
    lane = lax.broadcasted_iota(jnp.int32, (patches, patches), 1)
    first, second = order_ref[0], order_ref[1]
    position = jnp.where(place < rows, first * rows + place, second * rows + place - rows)
    chosen = lane == position
    route = jnp.sum(
        jnp.where(chosen, jnp.broadcast_to(route_ref[...], chosen.shape), 0).astype(F32),
        axis=1,
        keepdims=True,
    )
    perm[...] = (lane.astype(F32) == route).astype(BF16)
    req_lane = lax.broadcasted_iota(jnp.int32, (patches, req_total), 1)
    owner = jnp.zeros((patches, req_total), F32)
    start = jnp.int32(0)
    for q in range(req_total):
        end = start + len_ref[q]
        inside = (route >= start.astype(F32)) & (route < end.astype(F32))
        owner = jnp.where((req_lane == q) & inside, 1.0, owner)
        start = end
    pl.semaphore_wait(barrier, devices - 1)

    @pl.when(s == 0)
    def _():
        for step in range(1, reqs):
            lat_copy(step).start()
        lat[pl.ds(pl.multiple_of(r * own_rows, own_rows), own_rows), :] = latents_ref[...]

    same[...] = dot(owner, owner, ((1,), (1,)))
    chosen_bf = chosen.astype(F32).astype(BF16)
    stale = stale_ref[...].reshape(patches, heads * 2 * hd)
    stale = dot(chosen_bf[rows:, :], stale).astype(BF16)
    for h in range(heads):
        kv[h, rows:, :] = stale[:, h * 2 * hd : (h + 1) * 2 * hd]
    owner_bf = owner.astype(BF16)
    owners = jnp.concatenate([owner_bf, owner_bf, owner_bf], axis=1)

    def expand(table):
        high = table.astype(BF16)
        left = table - high.astype(F32)
        middle = left.astype(BF16)
        low = (left - middle.astype(F32)).astype(BF16)
        return dot(owners, jnp.concatenate([high, middle, low], axis=0))

    for k in (1, 2):
        for c in range(reqs):
            at = pl.ds(c * cols, cols)
            value = expand(mod_ref[k, :, at])
            mods[k - 1, :, at] = value + 1.0 if k == 1 else value

    def flatten(c, carry):
        raw_load(c).wait()
        at = pl.ds(pl.multiple_of(c * chunk, chunk), chunk)
        wq[at, :] = raw[at].reshape(chunk, heads * head_width)
        return carry

    lax.fori_loop(0, chunk_count, flatten, 0)
    loads[0].wait()
    qkv_width = heads * head_width
    group = 2 if heads % 2 == 0 else 1
    span = group * head_width
    piece = mlp_width // 3 if mlp_width % 384 == 0 else mlp_width
    qkv_parts = [(wq, at, span, at) for at in range(0, qkv_width, span)]
    mlp_parts = [(wi, at, piece, qkv_width + at) for at in range(0, mlp_width, piece)]
    lines = jnp.concatenate([mod_ref[1] + 1.0, mod_ref[0]], axis=0).astype(BF16)
    for weight, at, size, to in qkv_parts + mlp_parts:
        lined = dot(lines, weight[:, at : at + size])
        fixes[0, :, to : to + size] = expand(lined[:req_total])
        fixes[1, :, to : to + size] = expand(lined[req_total:])
    for load in loads[1:]:
        load.wait()

    @pl.when(s == 0)
    def _():
        for step in range(1, reqs):
            lat_copy(step).wait_recv()
        for c in range(reqs):
            entry = dot(perm[...], lat[:, c * cols : (c + 1) * cols]).astype(BF16)
            xin[0, c] = entry[:rows]
            xin[1, c] = entry[rows:]

    def x_copy(p, t, q, source):
        at = pl.ds(*pieces[p])
        return pltpu.make_async_remote_copy(
            src_ref=xnew.at[t, :, at],
            dst_ref=xin.at[t, source, :, at],
            send_sem=x_ssem.at[p, t, q],
            recv_sem=x_rsem.at[p, t, source],
            device_id=(lax.rem(s + 1, sections), q),
            device_id_type=MESH,
        )

    def part_copy(p, t, step):
        at = pl.ds(*pieces[p])
        return pltpu.make_async_remote_copy(
            src_ref=part_send.at[t, step, :, at],
            dst_ref=part_recv.at[t, step, :, at],
            send_sem=p_ssem.at[p, t, step],
            recv_sem=p_rsem.at[p, t, step],
            device_id=(s, peer(step)),
            device_id_type=MESH,
        )

    def slot(t, carry):
        at_rows = pl.ds(pl.multiple_of(t * rows, rows), rows)

        def push(p, part):
            begin, size = pieces[p]
            weight, at, part_size, _ = part
            return sum(
                dot(
                    normed[:, c * cols + begin : c * cols + begin + size],
                    weight[c * cols + begin : c * cols + begin + size, at : at + part_size],
                )
                for c in range(reqs)
            )

        stats = []
        base = None
        for p, (begin, size) in enumerate(pieces):
            for step in range(reqs):
                q = peer(step)

                @pl.when(s > 0)
                def _():
                    x_copy(p, t, q, q).wait_recv()

                value = xin[t, q, :, begin : begin + size].astype(F32)
                mean = jnp.sum(value, axis=1, keepdims=True) / size
                value = value - mean
                stats.append((size, mean, jnp.sum(value * value, axis=1, keepdims=True)))
            if base is None:
                base = sum(part for _, part, _ in stats) / reqs
            for c in range(reqs):
                at = pl.ds(c * cols + begin, size)
                value = xin[t, c, :, begin : begin + size].astype(F32) - base
                normed[:, at] = (value * mods[0, at_rows, at]).astype(BF16)
            if p < len(pieces) - 1:
                for part in qkv_parts + mlp_parts:
                    at = pl.ds(part[3], part[2])
                    pushed = push(p, part)
                    early[:, at] = pushed if p == 0 else early[:, at] + pushed
        mean = sum(size * part for size, part, _ in stats) / width
        square = sum(part + size * (at - mean) * (at - mean) for size, at, part in stats)
        scale = lax.rsqrt(square / width + 1e-06)
        offset = mean - base

        def product(part):
            at = pl.ds(part[3], part[2])
            value = push(len(pieces) - 1, part)
            if len(pieces) > 1:
                value = value + early[:, at]
            return (value - offset * fixes[0, at_rows, at]) * scale + fixes[1, at_rows, at]

        allowed = same[at_rows, :] > 0.5
        queries = []
        for g in range(heads // group):
            qkv = product(qkv_parts[g])
            for h in range(group):
                begin = h * head_width
                queries.append(qkv[:, begin : begin + hd].astype(BF16))
                fresh = qkv[:, begin + hd : begin + head_width].astype(BF16)
                kv[g * group + h, at_rows, :] = fresh

        chunks = len(mlp_parts)

        def up(c):
            return product(mlp_parts[c])

        def keep(c, hidden):
            at = attn_width + c * piece
            act[:, at : at + piece] = gelu_tanh(hidden).astype(BF16)

        scores = [dot(queries[h], kv[h, :, :hd], ((1,), (1,))) for h in range(heads)]
        hidden = up(0)
        attention = []
        for h in range(heads):
            score = jnp.where(allowed, scores[h] * (hd**-0.5), -jnp.inf)
            top = jnp.max(score, axis=1, keepdims=True)
            weights = jnp.exp(score - top)
            weights = weights / jnp.sum(weights, axis=1, keepdims=True)
            attention.append(weights.astype(BF16))
        keep(0, hidden)
        for c in range(1, chunks):
            hidden = up(c)
            if c == 1:
                for h in range(heads):
                    act[:, h * hd : (h + 1) * hd] = dot(attention[h], kv[h, :, hd:]).astype(BF16)
            keep(c, hidden)
        if chunks == 1:
            for h in range(heads):
                act[:, h * hd : (h + 1) * hd] = dot(attention[h], kv[h, :, hd:]).astype(BF16)

        def share(p, steps):
            begin, size = pieces[p]
            ats = [pl.ds(pl.multiple_of(peer(m) * cols + begin, 128), size) for m in steps]
            taken = [wo[:, at] for at in ats]
            taken = jnp.concatenate(taken, axis=1) if len(steps) > 1 else taken[0]
            shares = dot(act[...], taken).astype(BF16)
            for m, step in enumerate(steps):
                value = shares[:, m * size : (m + 1) * size]
                part_send[t, step, :, begin : begin + size] = value
                if step > 0:
                    part_copy(p, t, step).start()

        def update(p):
            begin, size = pieces[p]
            branch = part_send[t, 0, :, begin : begin + size].astype(F32)
            for step in range(1, reqs):
                part_copy(p, t, step).wait_recv()
                branch = branch + part_recv[t, step, :, begin : begin + size].astype(F32)
            own = pl.ds(pl.multiple_of(r * cols + begin, 128), size)
            gated = mods[1, at_rows, own] * branch
            updated = xin[t, r, :, begin : begin + size].astype(F32) + gated
            xnew[t, :, begin : begin + size] = updated.astype(BF16)

            @pl.when(s < sections - 1)
            def _():
                for step in range(reqs - 1, -1, -1):
                    x_copy(p, t, peer(step), r).start()

        together = 2 if reqs % 2 == 0 else 1
        turns = [
            (p, list(range(last, last - together, -1)))
            for p in range(len(pieces))
            for last in range(reqs - 1, -1, -together)
        ]
        updated = 0
        for n, (p, steps) in enumerate(turns):
            if n == len(turns) - 1 and len(pieces) > 1:
                update(0)
                updated = 1
            share(p, steps)
        for p in range(updated, len(pieces)):
            update(p)

        @pl.when(s == sections - 1)
        def _():
            xfin[at_rows, :] = xnew[t]

        return carry

    lax.fori_loop(0, 2, slot, 0)

    last_own = (sections - 1) // per
    is_self = (s == sections - 1) & (r == last_own)

    def fin_copy(u, q):
        return pltpu.make_async_remote_copy(
            src_ref=fin_send.at[u, q],
            dst_ref=fin_recv,
            send_sem=f_ssem.at[u, q],
            recv_sem=f_rsem.at[0],
            device_id=(r * per + u, q),
            device_id_type=MESH,
        )

    def to_self(u, q):
        return (r * per + u == sections - 1) & (r == q)

    @pl.when(s == sections - 1)
    def _():
        done = dot(perm[...], xfin[...], ((0,), (0,))).astype(BF16)
        out_cols = cols // per
        for u in range(per):
            for q in range(reqs):
                block = done[q * own_rows : (q + 1) * own_rows, u * out_cols : (u + 1) * out_cols]
                fin_send[u, q] = block

                @pl.when(to_self(u, q))
                def _():
                    out_ref[...] = block

                @pl.when(jnp.logical_not(to_self(u, q)))
                def _():
                    fin_copy(u, q).start()

    @pl.when(jnp.logical_not(is_self))
    def _():
        fin_copy(0, 0).wait_recv()
        out_ref[...] = fin_recv[...]

    @pl.when(s == sections - 1)
    def _():
        for u in range(per):
            for q in range(reqs):

                @pl.when(jnp.logical_not(to_self(u, q)))
                def _():
                    fin_copy(u, q).wait_send()

    @pl.when(s == 0)
    def _():
        for step in range(1, reqs):
            lat_copy(step).wait_send()

    for p in range(len(pieces)):
        for t in range(2):
            for step in range(1, reqs):
                part_copy(p, t, step).wait_send()

    @pl.when(s < sections - 1)
    def _():
        for p in range(len(pieces)):
            for t in range(2):
                for q in range(reqs):
                    x_copy(p, t, q, r).wait_send()


def relay_shards(
    latents,
    patch_route,
    request_len,
    span_order,
    modulation,
    w_qkv,
    w_mlp_in,
    w_out_attn,
    w_out_mlp,
    stale_kv,
):
    sections = lax.axis_size("section")
    reqs = lax.axis_size("req")
    patches = patch_route.shape[0]
    own_rows, width = latents.shape
    heads, head_width = w_qkv.shape[2:]
    hd = head_width // 3
    mlp_width = w_mlp_in.shape[2]
    rows, cols, per = patches // 2, width // reqs, sections // reqs
    out_cols = width // sections
    vmem = pl.BlockSpec(memory_space=pltpu.VMEM)
    smem = pl.BlockSpec(memory_space=pltpu.SMEM)
    hbm = pl.BlockSpec(memory_space=pl.ANY)
    weights = width * (heads * head_width + mlp_width) + (heads * hd + mlp_width) * width
    return pl.pallas_call(
        functools.partial(relay_kernel, sections, reqs),
        out_shape=jax.ShapeDtypeStruct((own_rows, out_cols), BF16),
        in_specs=[vmem, smem, smem, vmem, vmem, vmem, hbm, hbm, hbm, hbm],
        out_specs=vmem,
        scratch_shapes=[
            pltpu.VMEM((width, heads, head_width), BF16),
            pltpu.VMEM((width, heads * head_width), BF16),
            pltpu.VMEM((width, mlp_width), BF16),
            pltpu.VMEM((heads * hd + mlp_width, width), BF16),
            pltpu.VMEM((patches, width), BF16),
            pltpu.VMEM((2, reqs, rows, cols), BF16),
            pltpu.VMEM((rows, width), BF16),
            pltpu.VMEM((rows, heads * hd + mlp_width), BF16),
            pltpu.VMEM((heads, patches, 2 * hd), BF16),
            pltpu.VMEM((patches, patches), F32),
            pltpu.VMEM((patches, patches), BF16),
            pltpu.VMEM((2, patches, width), F32),
            pltpu.VMEM((2, patches, heads * head_width + mlp_width), F32),
            pltpu.VMEM((rows, heads * head_width + mlp_width), F32),
            pltpu.VMEM((2, reqs, rows, cols), BF16),
            pltpu.VMEM((2, reqs, rows, cols), BF16),
            pltpu.VMEM((2, rows, cols), BF16),
            pltpu.VMEM((patches, cols), BF16),
            pltpu.VMEM((per, reqs, own_rows, out_cols), BF16),
            pltpu.VMEM((own_rows, out_cols), BF16),
            pltpu.SemaphoreType.DMA((3 + width // 256,)),
            pltpu.SemaphoreType.DMA((reqs,)),
            pltpu.SemaphoreType.DMA((reqs,)),
            pltpu.SemaphoreType.DMA((len(pieces_of(cols)), 2, reqs)),
            pltpu.SemaphoreType.DMA((len(pieces_of(cols)), 2, reqs)),
            pltpu.SemaphoreType.DMA((len(pieces_of(cols)), 2, reqs)),
            pltpu.SemaphoreType.DMA((len(pieces_of(cols)), 2, reqs)),
            pltpu.SemaphoreType.DMA((per, reqs)),
            pltpu.SemaphoreType.DMA((1,)),
        ],
        compiler_params=pltpu.CompilerParams(
            collective_id=0, has_side_effects=True, vmem_limit_bytes=58 * 2**20
        ),
        cost_estimate=pl.CostEstimate(
            flops=2 * patches * weights, bytes_accessed=2 * weights, transcendentals=0
        ),
    )(
        patch_route.reshape(1, patches),
        request_len,
        span_order,
        latents,
        jnp.transpose(modulation[0], (1, 0, 2)),
        stale_kv[0],
        w_qkv[0],
        w_mlp_in[0],
        w_out_attn[0].reshape(heads * hd, width),
        w_out_mlp[0],
    )


def shards(*arrays):
    sections, reqs = lax.axis_size("section"), lax.axis_size("req")
    width, patches = arrays[0].shape[1], arrays[1].shape[0]
    fits = (
        arrays[3].shape[0] == 2
        and sections % reqs == 0
        and width % (sections * 128) == 0
        and patches % (reqs * 16) == 0
    )
    return (relay_shards if fits else plain_shards)(*arrays)


def solution(mesh):
    in_specs = (
        P("req", None),
        P(),
        P(),
        P(),
        P("section", None, None, None),
        P("section", None, "req", None),
        P("section", None, "req"),
        P("section", "req", None, None),
        P("section", "req", None),
        P("section", None, "req", None),
    )
    out_specs = P("req", "section")
    return jax.shard_map(shards, mesh=mesh, in_specs=in_specs, out_specs=out_specs, check_vma=False)
```

```python
import functools

import jax
import jax.numpy as jnp
from jax import lax
from jax.experimental import pallas as pl
from jax.experimental.pallas import tpu as pltpu
from jax.sharding import PartitionSpec as P


def from_behind(block, axis, distance):
    devices = range(lax.axis_size(axis))
    route = [(i - distance, i) for i in devices if i - distance in devices]
    return lax.ppermute(block, axis, route)


def spread_2(value, axis, source):
    kept = jnp.where(lax.axis_index(axis) == source, value, 0).astype(value.dtype)
    return lax.psum(kept, axis)


def layer_norm(values):
    row_mean = jnp.mean(values, axis=-1, keepdims=True)
    centered = values - row_mean
    row_var = jnp.mean(centered * centered, axis=-1, keepdims=True)
    return centered * lax.rsqrt(row_var + 1e-06)


def gelu_tanh(values):
    return (
        0.5
        * values
        * (1.0 + jnp.tanh(0.7978845608028654 * (values + 0.044715 * values * values * values)))
    )


def plain_shards(
    latents,
    patch_route,
    request_len,
    span_order,
    modulation,
    w_qkv,
    w_mlp_in,
    w_out_attn,
    w_out_mlp,
    stale_kv,
):
    section_count = lax.axis_size("section")
    req_count = lax.axis_size("req")
    section_index = lax.axis_index("section")
    req_index = lax.axis_index("req")
    patches = patch_route.shape[0]
    span_count = span_order.shape[0]
    span_rows = patches // span_count
    model_width = latents.shape[1]
    col_width = model_width // req_count
    section_cols = model_width // section_count
    req_total = request_len.shape[0]
    heads_dev = w_qkv.shape[2]
    head_dim = w_qkv.shape[3] // 3
    starts = jnp.cumsum(request_len) - request_len
    patch_ids = jnp.arange(patches, dtype=jnp.int32)
    owner_req = jnp.sum((patch_ids[:, None] >= starts[None, :]).astype(jnp.int32), axis=1) - 1
    seq_req = owner_req[patch_route]
    req_ids = jnp.arange(req_total, dtype=jnp.int32)
    mod_table = modulation[0].reshape(req_total, 3 * model_width)
    qkv_weight = w_qkv[0].reshape(model_width, heads_dev * 3 * head_dim)
    mlp_weight = w_mlp_in[0]
    attn_out_weight = w_out_attn[0].reshape(heads_dev * head_dim, model_width)
    mlp_out_weight = w_out_mlp[0]
    spread = lax.all_to_all(latents, "req", split_axis=1, concat_axis=0, tiled=True)
    sequence = spread[patch_route]
    in_width = sequence.shape[1]

    def work(incoming, kv_cache, span_id):
        first_row = span_id * span_rows
        row_req = lax.dynamic_slice_in_dim(seq_req, first_row, span_rows, 0)
        onehot = (row_req[:, None] == req_ids[None, :]).astype(jnp.float32)
        mod_rows = jnp.dot(onehot, mod_table, precision=lax.Precision.HIGHEST).reshape(
            span_rows, 3, model_width
        )
        current = lax.all_gather(incoming, "req", axis=1, tiled=True)
        normed = (
            layer_norm(current.astype(jnp.float32)) * (1.0 + mod_rows[:, 1]) + mod_rows[:, 0]
        ).astype(jnp.bfloat16)
        qkv_rows = jnp.dot(normed, qkv_weight, preferred_element_type=jnp.float32).reshape(
            span_rows, heads_dev, 3 * head_dim
        )
        query_rows = qkv_rows[:, :, :head_dim].astype(jnp.bfloat16)
        fresh_kv = qkv_rows[:, :, head_dim:].astype(jnp.bfloat16)
        kv_cache = lax.dynamic_update_slice_in_dim(kv_cache, fresh_kv, first_row, 0)
        key_rows = kv_cache[:, :, :head_dim]
        value_rows = kv_cache[:, :, head_dim:]
        scores = jnp.einsum(
            "chd,phd->hcp", query_rows, key_rows, preferred_element_type=jnp.float32
        ) / jnp.sqrt(jnp.float32(head_dim))
        same_req = row_req[:, None] == seq_req[None, :]
        scores = jnp.where(same_req[None], scores, -jnp.inf)
        row_top = jnp.max(scores, axis=-1, keepdims=True)
        weights = jnp.exp(scores - row_top)
        weight_sum = jnp.sum(weights, axis=-1, keepdims=True)
        attention = (weights / weight_sum).astype(jnp.bfloat16)
        attended = jnp.einsum(
            "hcp,phd->chd", attention, value_rows, preferred_element_type=jnp.float32
        ).astype(jnp.bfloat16)
        attended = attended.reshape(span_rows, heads_dev * head_dim)
        mlp_act = gelu_tanh(jnp.dot(normed, mlp_weight, preferred_element_type=jnp.float32)).astype(
            jnp.bfloat16
        )
        partial_value = jnp.dot(attended, attn_out_weight, preferred_element_type=jnp.float32)
        partial_value = partial_value + jnp.dot(
            mlp_act, mlp_out_weight, preferred_element_type=jnp.float32
        )
        branch = lax.psum_scatter(
            partial_value.astype(jnp.bfloat16), "req", scatter_dimension=1, tiled=True
        ).astype(jnp.float32)
        gate_cols = lax.dynamic_slice_in_dim(mod_rows[:, 2], req_index * col_width, col_width, 1)
        updated = (incoming.astype(jnp.float32) + gate_cols * branch).astype(jnp.bfloat16)
        return (updated, kv_cache)

    def advance(moment, carry):
        incoming, kv_cache, results = carry
        span_slot = moment - section_index
        active = (span_slot >= 0) & (span_slot < span_count)
        span_id = span_order[jnp.clip(span_slot, 0, span_count - 1)]
        first_row = span_id * span_rows
        entering = lax.dynamic_slice_in_dim(sequence, first_row, span_rows, 0)
        source = jnp.where(section_index == 0, entering, incoming)
        computed, new_cache = work(source, kv_cache, span_id)
        updated = jnp.where(active, computed, jnp.zeros_like(computed))
        kv_cache = jnp.where(active, new_cache, kv_cache)
        store_here = active & (section_index == section_count - 1)
        current = lax.dynamic_slice_in_dim(results, first_row, span_rows, 0)
        results = lax.dynamic_update_slice_in_dim(
            results, jnp.where(store_here, updated, current), first_row, 0
        )
        incoming = from_behind(updated, "section", 1)
        return (incoming, kv_cache, results)

    start_state = (
        jnp.zeros((span_rows, in_width), jnp.bfloat16),
        stale_kv[0],
        jnp.zeros((patches, in_width), jnp.bfloat16),
    )
    last_in, last_cache, results = lax.fori_loop(
        0, span_count + section_count - 1, advance, start_state
    )
    finished = spread_2(results, "section", section_count - 1)
    inverse = jnp.zeros((patches,), jnp.int32).at[patch_route].set(patch_ids)
    unrouted = finished[inverse]
    owned = lax.all_to_all(unrouted, "req", split_axis=0, concat_axis=1, tiled=True)
    return lax.dynamic_slice_in_dim(owned, section_index * section_cols, section_cols, 1)


MESH = pl.DeviceIdType.MESH
F32 = jnp.float32
BF16 = jnp.bfloat16


def dot(left, right, dims=((1,), (0,)), precision=None):
    return lax.dot_general(
        left, right, (dims, ((), ())), precision=precision, preferred_element_type=F32
    )


def pieces_of(cols):
    size = 256 if cols % 256 == 0 else cols
    return [(begin, size) for begin in range(0, cols, size)]


def relay_kernel(
    sections,
    reqs,
    route_ref,
    len_ref,
    order_ref,
    latents_ref,
    mod_ref,
    stale_ref,
    w_qkv_ref,
    w_in_ref,
    w_attn_ref,
    w_mlp_ref,
    out_ref,
    raw,
    wq,
    wi,
    wo,
    lat,
    xin,
    normed,
    act,
    kv,
    same,
    perm,
    mods,
    fixes,
    early,
    part_send,
    part_recv,
    xnew,
    xfin,
    fin_send,
    fin_recv,
    w_sem,
    lat_ssem,
    lat_rsem,
    x_ssem,
    x_rsem,
    p_ssem,
    p_rsem,
    f_ssem,
    f_rsem,
):
    s = lax.axis_index("section")
    r = lax.axis_index("req")
    devices = sections * reqs
    per = sections // reqs
    patches, width = lat.shape
    rows = patches // 2
    cols = width // reqs
    own_rows = patches // reqs
    heads, head_width = w_qkv_ref.shape[1:]
    chunk = 256
    chunk_count = width // chunk
    hd = head_width // 3
    pieces = pieces_of(cols)
    attn_width = heads * hd
    mlp_width = wi.shape[1]
    req_total = mod_ref.shape[1]

    def raw_load(c):
        at = pl.ds(pl.multiple_of(c * chunk, chunk), chunk)
        return pltpu.make_async_copy(w_qkv_ref.at[at], raw.at[at], w_sem.at[3 + c])

    for c in range(chunk_count):
        raw_load(c).start()
    loads = [
        pltpu.make_async_copy(w_in_ref, wi, w_sem.at[0]),
        pltpu.make_async_copy(w_attn_ref, wo.at[pl.ds(0, attn_width)], w_sem.at[1]),
        pltpu.make_async_copy(w_mlp_ref, wo.at[pl.ds(attn_width, mlp_width)], w_sem.at[2]),
    ]
    for load in loads:
        load.start()

    barrier = pltpu.get_barrier_semaphore()
    me = s * reqs + r

    def greet(step, carry):
        target = lax.rem(me + step, devices)
        pl.semaphore_signal(
            barrier,
            inc=1,
            device_id=(lax.div(target, reqs), lax.rem(target, reqs)),
            device_id_type=MESH,
        )
        return carry

    lax.fori_loop(1, devices, greet, 0)

    def peer(step):
        if reqs % 2:
            return lax.rem(r + step, reqs)
        across = lax.rem(lax.div(r, 2) + step // 2, reqs // 2)
        return across * 2 + lax.rem(r + step, 2)

    def lat_copy(step):
        mine = lat.at[pl.ds(pl.multiple_of(r * own_rows, own_rows), own_rows)]
        return pltpu.make_async_remote_copy(
            src_ref=latents_ref,
            dst_ref=mine,
            send_sem=lat_ssem.at[step],
            recv_sem=lat_rsem.at[step],
            device_id=(s, peer(step)),
            device_id_type=MESH,
        )

    place = lax.broadcasted_iota(jnp.int32, (patches, patches), 0)
    lane = lax.broadcasted_iota(jnp.int32, (patches, patches), 1)
    first, second = order_ref[0], order_ref[1]
    position = jnp.where(place < rows, first * rows + place, second * rows + place - rows)
    chosen = lane == position
    route = jnp.sum(
        jnp.where(chosen, jnp.broadcast_to(route_ref[...], chosen.shape), 0).astype(F32),
        axis=1,
        keepdims=True,
    )
    perm[...] = (lane.astype(F32) == route).astype(BF16)
    req_lane = lax.broadcasted_iota(jnp.int32, (patches, req_total), 1)
    owner = jnp.zeros((patches, req_total), F32)
    start = jnp.int32(0)
    for q in range(req_total):
        end = start + len_ref[q]
        inside = (route >= start.astype(F32)) & (route < end.astype(F32))
        owner = jnp.where((req_lane == q) & inside, 1.0, owner)
        start = end
    pl.semaphore_wait(barrier, devices - 1)

    @pl.when(s == 0)
    def _():
        for step in range(1, reqs):
            lat_copy(step).start()
        lat[pl.ds(pl.multiple_of(r * own_rows, own_rows), own_rows), :] = latents_ref[...]

    same[...] = dot(owner, owner, ((1,), (1,)))
    chosen_bf = chosen.astype(F32).astype(BF16)
    stale = stale_ref[...].reshape(patches, heads * 2 * hd)
    stale = dot(chosen_bf[rows:, :], stale).astype(BF16)
    for h in range(heads):
        kv[h, rows:, :] = stale[:, h * 2 * hd : (h + 1) * 2 * hd]
    owner_bf = owner.astype(BF16)
    owners = jnp.concatenate([owner_bf, owner_bf, owner_bf], axis=1)

    def expand(table):
        high = table.astype(BF16)
        left = table - high.astype(F32)
        middle = left.astype(BF16)
        low = (left - middle.astype(F32)).astype(BF16)
        return dot(owners, jnp.concatenate([high, middle, low], axis=0))

    for k in (1, 2):
        for c in range(reqs):
            at = pl.ds(c * cols, cols)
            value = expand(mod_ref[k, :, at])
            mods[k - 1, :, at] = value + 1.0 if k == 1 else value

    def flatten(c, carry):
        raw_load(c).wait()
        at = pl.ds(pl.multiple_of(c * chunk, chunk), chunk)
        wq[at, :] = raw[at].reshape(chunk, heads * head_width)
        return carry

    lax.fori_loop(0, chunk_count, flatten, 0)
    loads[0].wait()
    qkv_width = heads * head_width
    group = 2 if heads % 2 == 0 else 1
    span = group * head_width
    piece = mlp_width // 3 if mlp_width % 384 == 0 else mlp_width
    qkv_parts = [(wq, at, span, at) for at in range(0, qkv_width, span)]
    mlp_parts = [(wi, at, piece, qkv_width + at) for at in range(0, mlp_width, piece)]
    lines = jnp.concatenate([mod_ref[1] + 1.0, mod_ref[0]], axis=0).astype(BF16)
    for weight, at, size, to in qkv_parts + mlp_parts:
        lined = dot(lines, weight[:, at : at + size])
        fixes[0, :, to : to + size] = expand(lined[:req_total])
        fixes[1, :, to : to + size] = expand(lined[req_total:])
    for load in loads[1:]:
        load.wait()

    @pl.when(s == 0)
    def _():
        for step in range(1, reqs):
            lat_copy(step).wait_recv()
        for c in range(reqs):
            entry = dot(perm[...], lat[:, c * cols : (c + 1) * cols]).astype(BF16)
            xin[0, c] = entry[:rows]
            xin[1, c] = entry[rows:]

    def x_copy(p, t, q, source):
        at = pl.ds(*pieces[p])
        return pltpu.make_async_remote_copy(
            src_ref=xnew.at[t, :, at],
            dst_ref=xin.at[t, source, :, at],
            send_sem=x_ssem.at[p, t, q],
            recv_sem=x_rsem.at[p, t, source],
            device_id=(lax.rem(s + 1, sections), q),
            device_id_type=MESH,
        )

    def part_copy(p, t, step):
        at = pl.ds(*pieces[p])
        return pltpu.make_async_remote_copy(
            src_ref=part_send.at[t, step, :, at],
            dst_ref=part_recv.at[t, step, :, at],
            send_sem=p_ssem.at[p, t, step],
            recv_sem=p_rsem.at[p, t, step],
            device_id=(s, peer(step)),
            device_id_type=MESH,
        )

    def slot(t, carry):
        at_rows = pl.ds(pl.multiple_of(t * rows, rows), rows)

        def push(p, part):
            begin, size = pieces[p]
            weight, at, part_size, _ = part
            return sum(
                dot(
                    normed[:, c * cols + begin : c * cols + begin + size],
                    weight[c * cols + begin : c * cols + begin + size, at : at + part_size],
                )
                for c in range(reqs)
            )

        stats = []
        base = None
        for p, (begin, size) in enumerate(pieces):
            for step in range(reqs):
                q = peer(step)

                @pl.when(s > 0)
                def _():
                    x_copy(p, t, q, q).wait_recv()

                value = xin[t, q, :, begin : begin + size].astype(F32)
                mean = jnp.sum(value, axis=1, keepdims=True) / size
                value = value - mean
                stats.append((size, mean, jnp.sum(value * value, axis=1, keepdims=True)))
            if base is None:
                base = sum(part for _, part, _ in stats) / reqs
            for c in range(reqs):
                at = pl.ds(c * cols + begin, size)
                value = xin[t, c, :, begin : begin + size].astype(F32) - base
                normed[:, at] = (value * mods[0, at_rows, at]).astype(BF16)
            if p < len(pieces) - 1:
                for part in qkv_parts + mlp_parts:
                    at = pl.ds(part[3], part[2])
                    pushed = push(p, part)
                    early[:, at] = pushed if p == 0 else early[:, at] + pushed
        mean = sum(size * part for size, part, _ in stats) / width
        square = sum(part + size * (at - mean) * (at - mean) for size, at, part in stats)
        scale = lax.rsqrt(square / width + 1e-06)
        offset = mean - base

        def product(part):
            at = pl.ds(part[3], part[2])
            value = push(len(pieces) - 1, part)
            if len(pieces) > 1:
                value = value + early[:, at]
            return (value - offset * fixes[0, at_rows, at]) * scale + fixes[1, at_rows, at]

        allowed = same[at_rows, :] > 0.5
        queries = []
        for g in range(heads // group):
            qkv = product(qkv_parts[g])
            for h in range(group):
                begin = h * head_width
                queries.append(qkv[:, begin : begin + hd].astype(BF16))
                fresh = qkv[:, begin + hd : begin + head_width].astype(BF16)
                kv[g * group + h, at_rows, :] = fresh

        chunks = len(mlp_parts)

        def up(c):
            return product(mlp_parts[c])

        def keep(c, hidden):
            at = attn_width + c * piece
            act[:, at : at + piece] = gelu_tanh(hidden).astype(BF16)

        scores = [dot(queries[h], kv[h, :, :hd], ((1,), (1,))) for h in range(heads)]
        hidden = up(0)
        attention = []
        for h in range(heads):
            score = jnp.where(allowed, scores[h] * (hd**-0.5), -jnp.inf)
            top = jnp.max(score, axis=1, keepdims=True)
            weights = jnp.exp(score - top)
            weights = weights / jnp.sum(weights, axis=1, keepdims=True)
            attention.append(weights.astype(BF16))
        keep(0, hidden)
        for c in range(1, chunks):
            hidden = up(c)
            if c == 1:
                for h in range(heads):
                    act[:, h * hd : (h + 1) * hd] = dot(attention[h], kv[h, :, hd:]).astype(BF16)
            keep(c, hidden)
        if chunks == 1:
            for h in range(heads):
                act[:, h * hd : (h + 1) * hd] = dot(attention[h], kv[h, :, hd:]).astype(BF16)

        def share(p, steps):
            begin, size = pieces[p]
            ats = [pl.ds(pl.multiple_of(peer(m) * cols + begin, 128), size) for m in steps]
            taken = [wo[:, at] for at in ats]
            taken = jnp.concatenate(taken, axis=1) if len(steps) > 1 else taken[0]
            shares = dot(act[...], taken).astype(BF16)
            for m, step in enumerate(steps):
                value = shares[:, m * size : (m + 1) * size]
                part_send[t, step, :, begin : begin + size] = value
                if step > 0:
                    part_copy(p, t, step).start()

        def update(p):
            begin, size = pieces[p]
            branch = part_send[t, 0, :, begin : begin + size].astype(F32)
            for step in range(1, reqs):
                part_copy(p, t, step).wait_recv()
                branch = branch + part_recv[t, step, :, begin : begin + size].astype(F32)
            own = pl.ds(pl.multiple_of(r * cols + begin, 128), size)
            gated = mods[1, at_rows, own] * branch
            updated = xin[t, r, :, begin : begin + size].astype(F32) + gated
            xnew[t, :, begin : begin + size] = updated.astype(BF16)

            @pl.when(s < sections - 1)
            def _():
                for step in range(reqs - 1, -1, -1):
                    x_copy(p, t, peer(step), r).start()

        together = 2 if reqs % 2 == 0 else 1
        turns = [
            (p, list(range(last, last - together, -1)))
            for p in range(len(pieces))
            for last in range(reqs - 1, -1, -together)
        ]
        updated = 0
        for n, (p, steps) in enumerate(turns):
            if n == len(turns) - 2 and len(pieces) > 2:
                update(0)
                updated = 1
            share(p, steps)
        for p in range(updated, len(pieces)):
            update(p)

        @pl.when(s == sections - 1)
        def _():
            xfin[at_rows, :] = xnew[t]

        return carry

    lax.fori_loop(0, 2, slot, 0)

    last_own = (sections - 1) // per
    is_self = (s == sections - 1) & (r == last_own)

    def fin_copy(u, q):
        return pltpu.make_async_remote_copy(
            src_ref=fin_send.at[u, q],
            dst_ref=fin_recv,
            send_sem=f_ssem.at[u, q],
            recv_sem=f_rsem.at[0],
            device_id=(r * per + u, q),
            device_id_type=MESH,
        )

    def to_self(u, q):
        return (r * per + u == sections - 1) & (r == q)

    @pl.when(s == sections - 1)
    def _():
        done = dot(perm[...], xfin[...], ((0,), (0,))).astype(BF16)
        out_cols = cols // per
        for u in range(per):
            for q in range(reqs):
                block = done[q * own_rows : (q + 1) * own_rows, u * out_cols : (u + 1) * out_cols]
                fin_send[u, q] = block

                @pl.when(to_self(u, q))
                def _():
                    out_ref[...] = block

                @pl.when(jnp.logical_not(to_self(u, q)))
                def _():
                    fin_copy(u, q).start()

    @pl.when(jnp.logical_not(is_self))
    def _():
        fin_copy(0, 0).wait_recv()
        out_ref[...] = fin_recv[...]

    @pl.when(s == sections - 1)
    def _():
        for u in range(per):
            for q in range(reqs):

                @pl.when(jnp.logical_not(to_self(u, q)))
                def _():
                    fin_copy(u, q).wait_send()

    @pl.when(s == 0)
    def _():
        for step in range(1, reqs):
            lat_copy(step).wait_send()

    for p in range(len(pieces)):
        for t in range(2):
            for step in range(1, reqs):
                part_copy(p, t, step).wait_send()

    @pl.when(s < sections - 1)
    def _():
        for p in range(len(pieces)):
            for t in range(2):
                for q in range(reqs):
                    x_copy(p, t, q, r).wait_send()


def relay_shards(
    latents,
    patch_route,
    request_len,
    span_order,
    modulation,
    w_qkv,
    w_mlp_in,
    w_out_attn,
    w_out_mlp,
    stale_kv,
):
    sections = lax.axis_size("section")
    reqs = lax.axis_size("req")
    patches = patch_route.shape[0]
    own_rows, width = latents.shape
    heads, head_width = w_qkv.shape[2:]
    hd = head_width // 3
    mlp_width = w_mlp_in.shape[2]
    rows, cols, per = patches // 2, width // reqs, sections // reqs
    out_cols = width // sections
    vmem = pl.BlockSpec(memory_space=pltpu.VMEM)
    smem = pl.BlockSpec(memory_space=pltpu.SMEM)
    hbm = pl.BlockSpec(memory_space=pl.ANY)
    weights = width * (heads * head_width + mlp_width) + (heads * hd + mlp_width) * width
    return pl.pallas_call(
        functools.partial(relay_kernel, sections, reqs),
        out_shape=jax.ShapeDtypeStruct((own_rows, out_cols), BF16),
        in_specs=[vmem, smem, smem, vmem, vmem, vmem, hbm, hbm, hbm, hbm],
        out_specs=vmem,
        scratch_shapes=[
            pltpu.VMEM((width, heads, head_width), BF16),
            pltpu.VMEM((width, heads * head_width), BF16),
            pltpu.VMEM((width, mlp_width), BF16),
            pltpu.VMEM((heads * hd + mlp_width, width), BF16),
            pltpu.VMEM((patches, width), BF16),
            pltpu.VMEM((2, reqs, rows, cols), BF16),
            pltpu.VMEM((rows, width), BF16),
            pltpu.VMEM((rows, heads * hd + mlp_width), BF16),
            pltpu.VMEM((heads, patches, 2 * hd), BF16),
            pltpu.VMEM((patches, patches), F32),
            pltpu.VMEM((patches, patches), BF16),
            pltpu.VMEM((2, patches, width), F32),
            pltpu.VMEM((2, patches, heads * head_width + mlp_width), F32),
            pltpu.VMEM((rows, heads * head_width + mlp_width), F32),
            pltpu.VMEM((2, reqs, rows, cols), BF16),
            pltpu.VMEM((2, reqs, rows, cols), BF16),
            pltpu.VMEM((2, rows, cols), BF16),
            pltpu.VMEM((patches, cols), BF16),
            pltpu.VMEM((per, reqs, own_rows, out_cols), BF16),
            pltpu.VMEM((own_rows, out_cols), BF16),
            pltpu.SemaphoreType.DMA((3 + width // 256,)),
            pltpu.SemaphoreType.DMA((reqs,)),
            pltpu.SemaphoreType.DMA((reqs,)),
            pltpu.SemaphoreType.DMA((len(pieces_of(cols)), 2, reqs)),
            pltpu.SemaphoreType.DMA((len(pieces_of(cols)), 2, reqs)),
            pltpu.SemaphoreType.DMA((len(pieces_of(cols)), 2, reqs)),
            pltpu.SemaphoreType.DMA((len(pieces_of(cols)), 2, reqs)),
            pltpu.SemaphoreType.DMA((per, reqs)),
            pltpu.SemaphoreType.DMA((1,)),
        ],
        compiler_params=pltpu.CompilerParams(
            collective_id=0, has_side_effects=True, vmem_limit_bytes=58 * 2**20
        ),
        cost_estimate=pl.CostEstimate(
            flops=2 * patches * weights, bytes_accessed=2 * weights, transcendentals=0
        ),
    )(
        patch_route.reshape(1, patches),
        request_len,
        span_order,
        latents,
        jnp.transpose(modulation[0], (1, 0, 2)),
        stale_kv[0],
        w_qkv[0],
        w_mlp_in[0],
        w_out_attn[0].reshape(heads * hd, width),
        w_out_mlp[0],
    )


def shards(*arrays):
    sections, reqs = lax.axis_size("section"), lax.axis_size("req")
    width, patches = arrays[0].shape[1], arrays[1].shape[0]
    fits = (
        arrays[3].shape[0] == 2
        and sections % reqs == 0
        and width % (sections * 128) == 0
        and patches % (reqs * 16) == 0
    )
    return (relay_shards if fits else plain_shards)(*arrays)


def solution(mesh):
    in_specs = (
        P("req", None),
        P(),
        P(),
        P(),
        P("section", None, None, None),
        P("section", None, "req", None),
        P("section", None, "req"),
        P("section", "req", None, None),
        P("section", "req", None),
        P("section", None, "req", None),
    )
    out_specs = P("req", "section")
    return jax.shard_map(shards, mesh=mesh, in_specs=in_specs, out_specs=out_specs, check_vma=False)
```
